128 devices in a mesh: sx: 8 (over z, core), sy: 16 (over y, x).
Axes of the slice: x: 4, y: 4, z: 4, core: 2. Of those that a mesh axis runs over, the one named last changes fastest.
Arguments:
- jump_rhs: float32 [128, 2, 256, 512], P(('sx', 'sy')), may hold values from -12 to 12
- counts: int32 [128, 4], P(('sx', 'sy')), may hold values from 0 to 256, as said below
- slot_dof: int32 [128, 1024], P(('sx', 'sy')), may hold values from 0 to 1023, each once within a row
- remainder_inv: float32 [128, 1024, 1024], P(('sx', 'sy')), may hold values from -4 to 7, as said below
- schur_matrix: float32 [128, 1024, 1024], P(('sx', 'sy')), may hold values from -4 to 7, as said below
- coupling: float32 [128, 24, 1024], P(('sx', 'sy')), may hold values from -0.9 to 0.9
- coarse_local: float32 [128, 24, 24], P(('sx', 'sy')), may hold values from -4 to 7, as said below
- corner_map: int32 [128, 24], P(('sx', 'sy')), may hold values from 0 to 917, as said below
Outputs:
- multipliers: float32 [128, 2, 256, 512], P(('sx', 'sy'))
- residual: float32 [128, 2, 256, 512], P(('sx', 'sy'))
The draws below stay inside these ranges and needn't reach their ends.
Inputs may be any that keep to these rules, and one draw needn't show every extreme that they name: counts toward the outside of the grid are 0; a subdomain's west count equals its west neighbour's east count and its north count its north neighbour's south count; inside the grid counts run from 64 to 256. `corner_map`: each coarse degree of freedom belongs to a vertex of the subdomain grid and is named by the one to four subdomains that touch that vertex, never twice by one subdomain. `remainder_inv`: each subdomain's matrix is symmetric positive definite. `schur_matrix`: each subdomain's matrix is symmetric positive definite. `coarse_local`: each subdomain's matrix is symmetric positive definite.
All inputs are finite; a program needn't handle non-finite values.
Results may differ from the reference program's by a relative error of at most 0.00017.
Values sent between devices are 32-bit elements; how exact they have to be, the bound alone decides.
No kernel may reach another device: no remote copies, remote signals or barrier semaphores. Data moves between devices by JAX's collectives and lax.ppermute only.
A program may use at most 128 MiB of HBM per device.

```python
import jax
import jax.numpy as jnp
from jax import lax

NI = 1024
COMP = 3
NCL = 24
R = 512
ITERS = 2
CAP = 256
SUBDOMAIN_ROWS = 8
SUB_COLS = 16
SUBS = 128
COARSE_DOFS = 918


def gram_definite(key, count, order, strength, diag_low, upper_diagonal):
    leading_key, second_key = jax.random.split(key)
    block_keys = jax.random.split(leading_key, count)

    def one_block(block_key):
        factor_rows = jax.random.uniform(block_key, (order, order), jnp.float32, -1.0, 1.0)
        gram = jnp.dot(factor_rows, factor_rows.T, precision=lax.Precision.HIGHEST) * (strength / order)
        return 0.5 * (gram + gram.T)
    grams = lax.map(one_block, block_keys)
    diagonal = jax.random.uniform(second_key, (count, order), jnp.float32, diag_low, upper_diagonal)
    row_ids = lax.broadcasted_iota(jnp.int32, (order, order), 0)
    col_ids = lax.broadcasted_iota(jnp.int32, (order, order), 1)
    return grams + jnp.where((row_ids == col_ids)[None], diagonal[:, :, None], 0.0)


def draw_jump_rhs(key, part):
    key = jax.random.fold_in(key, 11)
    ramp = (3.0 ** (jnp.arange(SUBS, dtype=jnp.float32) / (SUBS - 1))).reshape(SUBS, 1, 1, 1)
    values = jnp.clip(jax.random.normal(key, (SUBS, 2, CAP, R), jnp.float32), -4.0, 4.0) * ramp
    return values


def draw_counts(key, part):
    key = jax.random.fold_in(key, 12)
    leading_key, second_key = jax.random.split(key)
    col_ids = lax.broadcasted_iota(jnp.int32, (SUBDOMAIN_ROWS, SUB_COLS), 1)
    row_ids = lax.broadcasted_iota(jnp.int32, (SUBDOMAIN_ROWS, SUB_COLS), 0)
    east = jax.random.randint(leading_key, (SUBDOMAIN_ROWS, SUB_COLS), CAP // 4, CAP + 1).astype(jnp.int32)
    east = jnp.where(col_ids == SUB_COLS - 1, 0, east.at[0, 0].set(CAP))
    south = jax.random.randint(second_key, (SUBDOMAIN_ROWS, SUB_COLS), CAP // 4, CAP + 1).astype(jnp.int32)
    south = jnp.where(row_ids == SUBDOMAIN_ROWS - 1, 0, south.at[0, 0].set(CAP))
    west = jnp.concatenate([jnp.zeros((SUBDOMAIN_ROWS, 1), jnp.int32), east[:, :-1]], 1)
    north = jnp.concatenate([jnp.zeros((1, SUB_COLS), jnp.int32), south[:-1]], 0)
    return jnp.stack([east, south, west, north], -1).reshape(SUBS, 4).astype(jnp.int32)


def draw_remainder_inv(key, part):
    key = jax.random.fold_in(key, 13)
    return gram_definite(key, SUBS, NI, 3.0, 0.5, 2.0)


def draw_schur_matrix(key, part):
    key = jax.random.fold_in(key, 14)
    return gram_definite(key, SUBS, NI, 3.0, 0.5, 2.0)


def draw_coarse_local(key, part):
    key = jax.random.fold_in(key, 15)
    return gram_definite(key, SUBS, NCL, 3.0, 0.5, 2.0)


def draw_corner_map(key, part):
    key = jax.random.fold_in(key, 16)
    leading_key, second_key = jax.random.split(key)
    vertex_rows = SUBDOMAIN_ROWS + 1
    vertex_cols = SUB_COLS + 1
    relabel_indices = jax.random.permutation(leading_key, COARSE_DOFS).astype(jnp.int32)
    sub_ids = jnp.arange(SUBS, dtype=jnp.int32)
    grid_row = sub_ids // SUB_COLS
    grid_col = sub_ids % SUB_COLS
    local_ids = jnp.arange(NCL, dtype=jnp.int32)
    component = local_ids % COMP
    vertex = local_ids // COMP
    layer = vertex // 4
    lower = vertex // 2 % 2
    right = vertex % 2
    point = (layer[None, :] * vertex_rows + grid_row[:, None] + lower[None, :]) * vertex_cols + grid_col[:, None] + right[None, :]
    natural = (point * COMP + component[None, :]).astype(jnp.int32)
    orders = jax.vmap(lambda one_key: jax.random.permutation(one_key, NCL))(jax.random.split(second_key, SUBS)).astype(jnp.int32)
    permuted_entries = jnp.take_along_axis(natural, orders, 1)
    return relabel_indices[permuted_entries].astype(jnp.int32)


def levels(key, extent, pieces, low, top_value):
    loudness, own = 1.0, jax.random.fold_in(key, 6)
    for position, parts in pieces:
        draws = jnp.exp(jax.random.uniform(jax.random.fold_in(own, position), (parts,), jnp.float32, low / len(pieces), top_value / len(pieces)))
        loudness = loudness * jnp.repeat(draws, extent[position] // parts).reshape([-1 if axis == position else 1 for axis in range(len(extent))])
    return loudness


def gaussian(rng, shape, deviation, bound, cuts=(), kind=jnp.bfloat16):
    result = jax.random.normal(rng, shape, jnp.float32) * deviation
    if len(cuts) > 0:
        result = levels(rng, shape, cuts, -0.22, 0.18) * result
    return jnp.clip(result, min=-bound, max=bound).astype(kind)


def setup_inputs(seed: int = 0) -> dict:
    arg_keys = jax.random.split(jax.random.key(seed), 9)
    return {
        "jump_rhs": draw_jump_rhs(jax.random.fold_in(arg_keys[8], 71), 0),
        "counts": draw_counts(jax.random.fold_in(arg_keys[8], 71), 0),
        "slot_dof": jax.vmap(lambda own: jax.random.permutation(own, NI))(jax.random.split(arg_keys[2], SUBS)).reshape((SUBS, NI)).astype(jnp.int32),
        "remainder_inv": draw_remainder_inv(jax.random.fold_in(arg_keys[8], 71), 0),
        "schur_matrix": draw_schur_matrix(jax.random.fold_in(arg_keys[8], 71), 0),
        "coupling": gaussian(arg_keys[5], (SUBS, NCL, NI), 0.15, 0.9, ((0, 128),), jnp.float32),
        "coarse_local": draw_coarse_local(jax.random.fold_in(arg_keys[8], 71), 0),
        "corner_map": draw_corner_map(jax.random.fold_in(arg_keys[8], 71), 0),
    }


highest = lax.Precision.HIGHEST

def triangle_solve(factor, loads):
    midpoint_split = lax.linalg.triangular_solve(factor, loads, left_side=True, lower=True)
    return lax.linalg.triangular_solve(factor, midpoint_split, left_side=True, lower=True, transpose_a=True)

def grid_shift(values, axis, offset):
    length = values.shape[axis]
    pad_shape = list(values.shape)
    pad_shape[axis] = abs(offset)
    padding = jnp.zeros(pad_shape, values.dtype)
    if offset > 0:
        return jnp.concatenate([padding, lax.slice_in_dim(values, 0, length - offset, axis=axis)], axis)
    return jnp.concatenate([lax.slice_in_dim(values, -offset, length, axis=axis), padding], axis)

def reference(jump_rhs, counts, slot_dof, remainder_inv, schur_matrix, coupling, coarse_local, corner_map):
    alive_mask = (jnp.arange(CAP, dtype=jnp.int32)[None, None, :] < counts[:, :, None]).astype(jnp.float32)[..., None]

    def spread(owned_values):
        grid_values = owned_values.reshape(SUBDOMAIN_ROWS, SUB_COLS, 2, CAP, R)
        from_west = grid_shift(grid_values[:, :, 0], 1, 1).reshape(SUBS, 1, CAP, R)
        from_north = grid_shift(grid_values[:, :, 1], 0, 1).reshape(SUBS, 1, CAP, R)
        slot_values = jnp.concatenate([owned_values, -from_west, -from_north], 1) * alive_mask
        slot_rows = slot_values.reshape(SUBS, NI, R)
        return jax.vmap(lambda rows_in, positions: jnp.zeros_like(rows_in).at[positions].set(rows_in))(slot_rows, slot_dof)

    def jump_values(dof_field):
        slot_values = jax.vmap(lambda rows_in, positions: rows_in[positions])(dof_field, slot_dof)
        slot_values = slot_values.reshape(SUBDOMAIN_ROWS, SUB_COLS, 4, CAP, R)
        from_east = grid_shift(slot_values[:, :, 2], 1, -1)
        from_south = grid_shift(slot_values[:, :, 3], 0, -1)
        jumped = jnp.stack([slot_values[:, :, 0] - from_east, slot_values[:, :, 1] - from_south], 2)
        return jumped.reshape(SUBS, 2, CAP, R) * alive_mask[:, :2]
    coarse_matrix = jnp.zeros((COARSE_DOFS, COARSE_DOFS), jnp.float32).at[corner_map[:, :, None], corner_map[:, None, :]].add(coarse_local)
    factor = jnp.linalg.cholesky(coarse_matrix)

    def operator(owned_values):
        spread_field = spread(owned_values)
        corner_load = jnp.einsum('scn,snr->scr', coupling, spread_field, precision=highest)
        placed = jnp.zeros((COARSE_DOFS, R), jnp.float32).at[corner_map.reshape(-1)].add(corner_load.reshape(SUBS * NCL, R))
        solved = triangle_solve(factor, placed)
        dof_field = jnp.einsum('snm,smr->snr', remainder_inv, spread_field, precision=highest)
        dof_field = dof_field + jnp.einsum('scn,scr->snr', coupling, solved[corner_map], precision=highest)
        return jump_values(dof_field)

    def precondition(owned_values):
        return jump_values(jnp.einsum('snm,smr->snr', schur_matrix, spread(owned_values), precision=highest))

    def inner_sum(former, latter):
        return jnp.sum(former * latter, axis=(0, 1, 2))
    residual = jump_rhs * alive_mask[:, :2]
    multipliers = jnp.zeros_like(residual)
    preconditioned = precondition(residual)
    direction = preconditioned
    residual_dot = inner_sum(residual, preconditioned)
    for iteration in range(ITERS):
        image = operator(direction)
        step_length = residual_dot / inner_sum(direction, image)
        multipliers = multipliers + step_length * direction
        residual = residual - step_length * image
        if iteration + 1 < ITERS:
            preconditioned = precondition(residual)
            dot_next = inner_sum(residual, preconditioned)
            direction = preconditioned + dot_next / residual_dot * direction
            residual_dot = dot_next
    return (multipliers, residual)
```

```python
import functools

import jax
import jax.numpy as jnp
from jax import lax
from jax.experimental import pallas as pl
from jax.experimental.pallas import tpu as pltpu
from jax.sharding import PartitionSpec as P

f32, bf16 = jnp.float32, jnp.bfloat16
highest = lax.Precision.HIGHEST
BOTH = ("sx", "sy")
CAP, R, NI = 256, 512, 1024
LEVELS = (
    (1, tuple(range(1, 16, 2))),
    (2, (2, 6, 10, 14)),
    (4, (4, 12)),
    (8, (0, 16)),
)
ROOT = 8
BLOCKS = 17
VM = pl.BlockSpec(memory_space=pltpu.VMEM)
SM = pl.BlockSpec(memory_space=pltpu.SMEM)


def call(body, ins, outs, scratch=(), specs=None):
    return pl.pallas_call(
        body,
        out_shape=[jax.ShapeDtypeStruct(s, d) for s, d in outs],
        in_specs=specs if specs is not None else [VM] * len(ins),
        out_specs=[VM] * len(outs),
        scratch_shapes=list(scratch),
        compiler_params=pltpu.CompilerParams(vmem_limit_bytes=48 * 1024 * 1024),
    )(*ins)


def dot(a, b):
    return jnp.dot(a, b, preferred_element_type=f32)


def split(x):
    hi = x.astype(bf16)
    return hi, (x - hi.astype(f32)).astype(bf16)


def iota(shape, axis):
    return lax.broadcasted_iota(jnp.int32, shape, axis)


def permute_body(mat, row_dof, col_dof, hi_out, lo_out):
    pick = jnp.where(iota((NI, NI), 1) == col_dof[...], 1.0, 0.0).astype(bf16)
    pick_t = jnp.where(iota((NI, NI), 0) == row_dof[...], 1.0, 0.0).astype(bf16)
    hi, lo = split(mat[...])
    for part, out in ((hi, hi_out), (lo, lo_out)):
        rows = dot(pick, part).astype(bf16)
        out[...] = dot(rows, pick_t).astype(bf16)


def coupling_body(coupling, order, row_dof, out, out_t):
    pick_t = jnp.where(iota((NI, NI), 0) == row_dof[...], 1.0, 0.0).astype(bf16)
    ranked = jnp.dot(order[...], coupling[...], precision=highest, preferred_element_type=f32)
    hi, lo = split(ranked)
    hi, lo = dot(hi, pick_t), dot(lo, pick_t)
    out[...] = jnp.concatenate([hi, lo], 0).astype(bf16)
    tall = jnp.concatenate([hi, hi, lo, jnp.zeros_like(lo)], 0)
    out_t[...] = tall.T.astype(bf16)


def neighbours(stride, pivot):
    left = pivot - stride if pivot - stride >= 0 else None
    right = pivot + stride if pivot + stride < BLOCKS else None
    return left, right


def coarse_body(rows, columns, x, dh, dl, gh, gl, diag, side):
    lane8 = iota((8, 128), 1)
    sub8 = iota((8, 128), 0)
    r0, c0 = iota((128, 128), 0), iota((128, 128), 1)
    start = jnp.where((r0 == c0) & (r0 % 8 >= 6) & (r0 < 72), 1.0, 0.0)
    for j in range(BLOCKS):
        diag[j] = start
        side[j] = jnp.zeros((128, 256), f32)

    def piece(tile, right_a, lower_a, right_b, r):
        offset = (right_a * 2 + lower_a) * 32 + right_b * 16
        moved = pltpu.roll(tile, (r * 8 - offset) % 128, 1)
        return jnp.where((lane8 >= r * 8) & (lane8 < r * 8 + 16), moved, 0.0)

    def gather(pair, _):
        for odd in (0, 1):
            c = pair * 2 + odd
            tiles = [x[pl.ds(pl.multiple_of((r * columns + c) * 8, 8), 8), :] for r in range(rows)]
            for right in (0, 1):
                for i in range(rows + 1):
                    acc = diag[c + right, i * 8 : i * 8 + 8, :]
                    for lower in (0, 1):
                        if 0 <= i - lower < rows:
                            acc = acc + piece(tiles[i - lower], right, lower, right, i - lower)
                    diag[c + right, i * 8 : i * 8 + 8, :] = acc
            right_a = 0 if odd else 1
            at = 128 if odd else 0
            for i in range(rows + 1):
                acc = jnp.zeros((8, 128), f32)
                for lower in (0, 1):
                    if 0 <= i - lower < rows:
                        acc = acc + piece(tiles[i - lower], right_a, lower, 1 - right_a, i - lower)
                side[pair * 2 + 1, i * 8 : i * 8 + 8, at : at + 128] = acc
        return 0

    lax.fori_loop(0, columns // 2, gather, 0)

    def invert(blocks):
        def vertex(i, _):
            inside = (lane8 >= i * 8) & (lane8 < i * 8 + 8)
            base = pl.multiple_of(i * 8, 8)
            for j in blocks:
                old = [diag[j, m * 8 : m * 8 + 8, :] for m in range(9)]
                turned = [pltpu.roll(t, 128 - i * 8, 1) for t in old]
                own = diag[j, pl.ds(base, 8), :]
                own_turned = pltpu.roll(own, 128 - i * 8, 1)
                panel = [jnp.broadcast_to(own_turned[:, p : p + 1], (8, 128)) for p in range(6)]
                wide = jnp.where(inside, jnp.where(lane8 - i * 8 == sub8, 1.0, 0.0), own)
                for p in range(6):
                    inverse = 1.0 / jnp.broadcast_to(panel[p][p : p + 1, :], (8, 128))
                    row = jnp.broadcast_to(wide[p : p + 1, :], (8, 128)) * inverse
                    wide = jnp.where(sub8 == p, row, wide - panel[p] * row)
                    for q in range(p + 1, 6):
                        row = jnp.broadcast_to(panel[q][p : p + 1, :], (8, 128)) * inverse
                        panel[q] = jnp.where(sub8 == p, row, panel[q] - panel[p] * row)
                spread_rows = [jnp.broadcast_to(wide[p : p + 1, :], (8, 128)) for p in range(6)]
                for m in range(9):
                    acc = jnp.where(inside, 0.0, old[m])
                    for p in range(6):
                        acc = acc - turned[m][:, p : p + 1] * spread_rows[p]
                    diag[j, m * 8 : m * 8 + 8, :] = acc
                diag[j, pl.ds(base, 8), :] = wide
            return 0

        lax.fori_loop(0, 9, vertex, 0)

    for level, (stride, pivots) in enumerate(LEVELS):
        invert(pivots)
        later = LEVELS[level + 1][1] if level + 1 < len(LEVELS) else ()
        for p in pivots:
            left, right = neighbours(stride, p)
            coupled = side[p]
            gain = jnp.dot(diag[p], coupled, precision=highest, preferred_element_type=f32)
            hi, lo = split(gain)
            gh[p] = hi
            gl[p] = lo
            schur = jnp.dot(coupled.T, gain, precision=highest, preferred_element_type=f32)
            if left is not None:
                diag[left] = diag[left] - schur[:128, :128]
            if right is not None:
                diag[right] = diag[right] - schur[128:, 128:]
            if left is not None and right is not None:
                if left in later:
                    side[left, :, 128:] = -schur[:128, 128:]
                else:
                    side[right, :, :128] = -schur[128:, :128]
    invert((ROOT,))
    gh[ROOT] = jnp.zeros((128, 256), bf16)
    gl[ROOT] = jnp.zeros((128, 256), bf16)
    for j in range(BLOCKS):
        hi, lo = split(diag[j])
        dh[j] = hi
        dl[j] = lo


def coarse_factor(blocks, rows, columns):
    return call(
        functools.partial(coarse_body, rows, columns),
        (blocks,),
        [
            ((BLOCKS, 128, 128), bf16),
            ((BLOCKS, 128, 128), bf16),
            ((BLOCKS, 128, 256), bf16),
            ((BLOCKS, 128, 256), bf16),
        ],
        [pltpu.VMEM((BLOCKS, 128, 128), f32), pltpu.VMEM((BLOCKS, 128, 256), f32)],
    )


def row_times(x, hi, lo, transposed=False):
    high = x.astype(bf16).astype(f32)
    both = jnp.concatenate([high, x - high], 0).astype(bf16)
    dims = (((1,), (1 if transposed else 0,)), ((), ()))
    out = lax.dot_general(both, hi, dims, preferred_element_type=f32)
    out = out + lax.dot_general(both, lo, dims, preferred_element_type=f32)
    return out[:8] + out[8:]


def coarse_solve(rows, columns, w, dh, dl, gh, gl, placed, solved):
    lane16 = iota((16, 128), 1)
    placed[...] = jnp.zeros_like(placed)
    solved[...] = jnp.zeros_like(solved)
    for k in range(4):
        for right in (0, 1):
            offset = k * 32 + right * 16
            acc = jnp.zeros((16, 128), f32)
            for r in range(rows):
                moved = pltpu.roll(w[r * columns : (r + 1) * columns, :], (r * 8 - offset) % 128, 1)
                take = (lane16 >= r * 8) & (lane16 < r * 8 + 16) & (lane16 % 8 < 6)
                acc = acc + jnp.where(take, moved, 0.0)
            at = k * 24 + right
            placed[at : at + 16, :] = placed[at : at + 16, :] + acc
    b = [placed[pl.ds(j, 8, stride=24), :] for j in range(BLOCKS)]
    none = jnp.zeros((8, 128), f32)
    y, sol = [none] * BLOCKS, [none] * BLOCKS
    for stride, pivots in LEVELS:
        for p in pivots:
            left, right = neighbours(stride, p)
            gb = row_times(b[p], gh[p], gl[p])
            if left is not None:
                b[left] = b[left] - gb[:, :128]
            if right is not None:
                b[right] = b[right] - gb[:, 128:]
            y[p] = row_times(b[p], dh[p], dl[p])
    sol[ROOT] = row_times(b[ROOT], dh[ROOT], dl[ROOT])
    for stride, pivots in LEVELS[::-1]:
        for p in pivots:
            left, right = neighbours(stride, p)
            pair = jnp.concatenate(
                [none if left is None else sol[left], none if right is None else sol[right]], 1
            )
            sol[p] = y[p] - row_times(pair, gh[p], gl[p], True)
    for j in range(BLOCKS):
        solved[pl.ds(j, 8, stride=24), :] = sol[j]
    product = placed[...] * solved[...]
    energy = [jnp.sum(product[k * 24 : k * 24 + 24, :], keepdims=True) for k in range(4)]
    answers = []
    for r in range(rows):
        acc = jnp.zeros((16, 128), f32)
        for k in range(4):
            for right in (0, 1):
                offset = k * 32 + right * 16
                at = k * 24 + right
                moved = pltpu.roll(solved[at : at + 16, :], (offset - r * 8) % 128, 1)
                acc = acc + jnp.where((lane16 >= offset) & (lane16 < offset + 16), moved, 0.0)
        answers.append(acc)
    return answers, energy


def lane_sum(total, at):
    lane = iota((1, 128), 1)
    return jnp.sum(jnp.where(lane == at, total, 0.0), axis=1, keepdims=True)


def by_case(values):
    lane = iota((1, 128), 1)
    out = jnp.zeros((1, 128), f32)
    for k in range(4):
        out = jnp.where(lane // 32 == k, values[k], out)
    return out


def write_answers(out, answers, columns, first, second):
    lane = iota((1, 128), 1)
    for r, acc in enumerate(answers):
        acc = jnp.where(lane % 32 == 6, first, acc)
        acc = jnp.where(lane % 32 == 7, second, acc)
        out[r * columns : (r + 1) * columns, :] = acc


def first_solve_body(rows, columns, w, dh, dl, gh, gl, out, state, placed, solved):
    answers, energy = coarse_solve(rows, columns, w, dh, dl, gh, gl, placed, solved)
    total = jnp.sum(w[...], axis=0, keepdims=True)
    dots = by_case([lane_sum(total, k * 32 + 6) for k in range(4)])
    curvature = by_case([lane_sum(total, k * 32 + 7) + energy[k] for k in range(4)])
    state[...] = jnp.concatenate([dots, curvature, jnp.zeros((6, 128), f32)], 0)
    step = dots / curvature
    write_answers(out, answers, columns, step, step)


def second_solve_body(rows, columns, w, state, dh, dl, gh, gl, out, placed, solved):
    answers, energy = coarse_solve(rows, columns, w, dh, dl, gh, gl, placed, solved)
    total = jnp.sum(w[...], axis=0, keepdims=True)
    dots = by_case([lane_sum(total, k * 32 + 6) for k in range(4)])
    own = by_case([lane_sum(total, k * 32 + 7) + energy[k] for k in range(4)])
    cross = by_case([lane_sum(total, k * 32 + 14) for k in range(4)])
    ratio = dots / state[0:1, :]
    curvature = own + ratio * (2.0 * cross + ratio * state[1:2, :])
    write_answers(out, answers, columns, dots / curvature, ratio)


def solve_scratch():
    return [pltpu.VMEM((192, 128), f32), pltpu.VMEM((192, 128), f32)]


def mask_of(counts, k):
    return iota((CAP, R), 0) < counts[k]


def product(hi, lo, x, k):
    a, b = hi[k * CAP : (k + 1) * CAP, :], lo[k * CAP : (k + 1) * CAP, :]
    xh, xl = x
    return dot(a, xh) + dot(a, xl) + dot(b, xh)


def start_body(counts, rhs, west, north, hi, lo, r4, *t):
    for k, (values, sign) in enumerate(((rhs[0], 1.0), (rhs[1], 1.0), (west[...], -1.0), (north[...], -1.0))):
        r4[k * CAP : (k + 1) * CAP, :] = jnp.where(mask_of(counts, k), values * sign, 0.0)
    x = split(r4[...])
    for k in range(4):
        t[k][...] = product(hi, lo, x, k)


def jumped(counts, t, received, k):
    return jnp.where(mask_of(counts, k), t[k][...] - received[k][...], 0.0)


def payload(loads, rows_of_dots):
    sub = iota((32, R), 0)
    for at, values in rows_of_dots:
        loads = jnp.where(sub == at, values, loads)
    tall = jnp.concatenate([loads[:, k * 128 : (k + 1) * 128] for k in range(4)], 0)
    return tall.T


def corner_loads(coupling, x):
    xh, xl = x
    both = dot(coupling[...], xh)
    return both[:32] + both[32:] + dot(coupling[:32, :], xl)


def sum_rows(x):
    return jnp.sum(x, axis=0, keepdims=True)


def operate(counts, t, received, hi, lo, coupling, field, u):
    for k in range(4):
        field[k * CAP : (k + 1) * CAP, :] = jumped(counts, t, received, k)
    x = split(field[...])
    loads = corner_loads(coupling, x)
    energy = jnp.zeros((1, R), f32)
    for k in range(4):
        part = product(hi, lo, x, k)
        u[k * CAP : (k + 1) * CAP, :] = part
        energy = energy + sum_rows(part * field[k * CAP : (k + 1) * CAP, :])
    return loads, energy


def first_operator_body(counts, t0, t1, t2, t3, e0, e1, e2, e3, r4, hi, lo, coupling, z4, u, out):
    loads, energy = operate(counts, (t0, t1, t2, t3), (e0, e1, e2, e3), hi, lo, coupling, z4, u)
    dots = sum_rows(r4[: 2 * CAP, :] * z4[: 2 * CAP, :])
    out[...] = payload(loads, ((6, dots), (7, energy)))


def second_operator_body(
    counts, t0, t1, t2, t3, e0, e1, e2, e3, r1, w4, hi, lo, coupling, z4, u, out
):
    loads, energy = operate(counts, (t0, t1, t2, t3), (e0, e1, e2, e3), hi, lo, coupling, z4, u)
    owned = z4[: 2 * CAP, :]
    dots = sum_rows(r1[...] * owned)
    cross = sum_rows(w4[...] * owned)
    out[...] = payload(loads, ((6, dots), (7, energy), (14, cross)))


def unpack(answer):
    tall = answer[...].T
    return jnp.concatenate([tall[k * 32 : (k + 1) * 32, :] for k in range(4)], 1)


def finish_body(u, answer, coupling_t, scalars, *t):
    flat = unpack(answer)
    scalars[...] = flat[0:8, :]
    flat = jnp.where(iota((32, R), 0) % 8 < 6, flat, 0.0)
    hi = flat.astype(bf16).astype(f32)
    lo = flat - hi
    tall = jnp.concatenate([hi, lo, hi, jnp.zeros_like(hi)], 0).astype(bf16)
    for k in range(4):
        rows = slice(k * CAP, (k + 1) * CAP)
        t[k][...] = u[rows, :] + dot(coupling_t[rows, :], tall)


def precondition_body(
    counts, t0, t1, t2, t3, e0, e1, e2, e3, r4, scalars, hi, lo, r1, w, s0, s1, s2, s3, work
):
    t, received = (t0, t1, t2, t3), (e0, e1, e2, e3)
    step = scalars[6:7, :]
    for k in range(4):
        rows = slice(k * CAP, (k + 1) * CAP)
        image = jumped(counts, t, received, k)
        if k < 2:
            w[rows, :] = image
        work[rows, :] = r4[rows, :] - step * image
        if k < 2:
            r1[rows, :] = work[rows, :]
    x = split(work[...])
    for k, out in enumerate((s0, s1, s2, s3)):
        out[...] = product(hi, lo, x, k)


def end_body(counts, t0, t1, e0, e1, z4, z1, r1, w, first, second, mult, residual):
    t, received = (t0, t1), (e0, e1)
    step, last, ratio = first[6:7, :], second[6:7, :], second[7:8, :]
    for k in range(2):
        rows = slice(k * CAP, (k + 1) * CAP)
        start = z4[rows, :]
        mult[k] = step * start + last * (z1[rows, :] + ratio * start)
        image = jumped(counts, t, received, k) + ratio * w[rows, :]
        residual[k] = r1[rows, :] - last * image


def shift(block, axis, distance):
    devices = range(lax.axis_size(axis))
    route = [(i - distance, i) for i in devices if i - distance in devices]
    return lax.ppermute(block, axis, route)


def exchange(t):
    return (
        shift(t[2], "sy", -1),
        shift(t[3], "sx", -1),
        shift(t[0], "sy", 1),
        shift(t[1], "sx", 1),
    )


def everywhere(blocks):
    return lax.all_to_all(blocks, BOTH, 0, 0, tiled=True)


def vertex_order(corner_map):
    names = corner_map[0]
    tags = names[None] + 1
    east, west = shift(tags, "sy", -1)[0], shift(tags, "sy", 1)[0]
    south, north = shift(tags, "sx", -1)[0], shift(tags, "sx", 1)[0]

    def named(other):
        return jnp.any(tags[0][:, None] == other[None, :], axis=1)

    last_column = lax.axis_index("sy") == lax.axis_size("sy") - 1
    last_row = lax.axis_index("sx") == lax.axis_size("sx") - 1
    right = jnp.where(last_column, ~named(west), named(east)).astype(jnp.int32)
    lower = jnp.where(last_row, ~named(north), named(south)).astype(jnp.int32)
    vertex = right * 2 + lower
    before = (vertex[:, None] == vertex[None, :]) & (names[None, :] < names[:, None])
    row = vertex * 8 + jnp.sum(before.astype(jnp.int32), axis=1)
    return (jnp.arange(32, dtype=jnp.int32)[:, None] == row[None, :]).astype(f32)


def on_device(
    jump_rhs, counts, slot_dof, remainder_inv, schur_matrix, coupling, coarse_local, corner_map
):
    rows, columns = lax.axis_size("sx"), lax.axis_size("sy")
    devices = rows * columns
    counts = counts[0]
    rhs = jump_rhs[0]
    west, north = shift(rhs[0], "sy", 1), shift(rhs[1], "sx", 1)
    order = vertex_order(corner_map)
    local = jnp.dot(jnp.dot(order, coarse_local[0], precision=highest), order.T, precision=highest)
    local = jnp.concatenate([local[v * 8 : v * 8 + 8] for v in range(4)], 1)
    blocks = everywhere(jnp.broadcast_to(local[None], (devices, 8, 128)))

    row_dof, col_dof = slot_dof, slot_dof.reshape(NI, 1)
    matrix_outs = [((NI, NI), bf16), ((NI, NI), bf16)]
    sh, sl = call(permute_body, (schur_matrix[0], row_dof, col_dof), matrix_outs)
    rh, rl = call(permute_body, (remainder_inv[0], row_dof, col_dof), matrix_outs)
    cpl, cpl_t = call(
        coupling_body, (coupling[0], order, row_dof), [((64, NI), bf16), ((NI, 128), bf16)]
    )
    factor = coarse_factor(blocks.reshape(devices * 8, 128), rows, columns)

    field, half, slab = ((NI, R), f32), ((2 * CAP, R), f32), ((CAP, R), f32)
    message, few = ((128, 128), f32), ((8, R), f32)
    specs = lambda n: [SM] + [VM] * n

    r4, *t = call(start_body, (counts, rhs, west, north, sh, sl), [field] + [slab] * 4, (), specs(5))
    received = exchange(t)
    z4, u, out = call(
        first_operator_body,
        (counts, *t, *received, r4, rh, rl, cpl),
        [field, field, message],
        (),
        specs(12),
    )
    answer, state = call(
        functools.partial(first_solve_body, rows, columns),
        (everywhere(out), *factor),
        [message, ((8, 128), f32)],
        solve_scratch(),
    )
    first, *t = call(finish_body, (u, everywhere(answer), cpl_t), [few] + [slab] * 4)
    received = exchange(t)
    r1, w, *t = call(
        precondition_body,
        (counts, *t, *received, r4, first, sh, sl),
        [half, half] + [slab] * 4,
        [pltpu.VMEM((NI, R), f32)],
        specs(12),
    )
    received = exchange(t)
    z1, u, out = call(
        second_operator_body,
        (counts, *t, *received, r1, w, rh, rl, cpl),
        [field, field, message],
        (),
        specs(13),
    )
    (answer,) = call(
        functools.partial(second_solve_body, rows, columns),
        (everywhere(out), state, *factor),
        [message],
        solve_scratch(),
    )
    second, *t = call(finish_body, (u, everywhere(answer), cpl_t), [few] + [slab] * 4)
    own = ((2, CAP, R), f32)
    multipliers, residual = call(
        end_body,
        (counts, t[0], t[1], shift(t[2], "sy", -1), shift(t[3], "sx", -1), z4, z1, r1, w, first, second),
        [own, own],
        (),
        specs(10),
    )
    return multipliers[None], residual[None]


def solution(mesh):
    four, three, two = P(BOTH, None, None, None), P(BOTH, None, None), P(BOTH, None)
    return jax.shard_map(
        on_device,
        mesh=mesh,
        in_specs=(four, two, two, three, three, three, three, two),
        out_specs=(four, four),
        check_vma=False,
    )
```

```python
import functools

import jax
import jax.numpy as jnp
from jax import lax
from jax.experimental import pallas as pl
from jax.experimental.pallas import tpu as pltpu
from jax.sharding import PartitionSpec as P

f32, bf16 = jnp.float32, jnp.bfloat16
highest = lax.Precision.HIGHEST
BOTH = ("sx", "sy")
CAP, R, NI = 256, 512, 1024
LEVELS = (
    (1, tuple(range(1, 16, 2))),
    (2, (2, 6, 10, 14)),
    (4, (4, 12)),
    (8, (0, 16)),
)
ROOT = 8
BLOCKS = 17
VM = pl.BlockSpec(memory_space=pltpu.VMEM)
SM = pl.BlockSpec(memory_space=pltpu.SMEM)


def call(body, ins, outs, scratch=(), specs=None, us=1.0, mib=24):
    return pl.pallas_call(
        body,
        out_shape=[jax.ShapeDtypeStruct(s, d) for s, d in outs],
        in_specs=specs if specs is not None else [VM] * len(ins),
        out_specs=[VM] * len(outs),
        scratch_shapes=list(scratch),
        cost_estimate=pl.CostEstimate(flops=int(us * 1.15e9), bytes_accessed=int(us * 1e6), transcendentals=0),
        compiler_params=pltpu.CompilerParams(vmem_limit_bytes=mib * 1024 * 1024),
    )(*ins)


def dot(a, b):
    return jnp.dot(a, b, preferred_element_type=f32)


def split(x):
    hi = x.astype(bf16)
    return hi, (x - hi.astype(f32)).astype(bf16)


def iota(shape, axis):
    return lax.broadcasted_iota(jnp.int32, shape, axis)


def permute_body(mat, row_dof, col_dof, hi_out, lo_out):
    pick = jnp.where(iota((NI, NI), 1) == col_dof[...], 1.0, 0.0).astype(bf16)
    pick_t = jnp.where(iota((NI, NI), 0) == row_dof[...], 1.0, 0.0).astype(bf16)
    hi, lo = split(mat[...])
    for part, out in ((hi, hi_out), (lo, lo_out)):
        rows = dot(pick, part).astype(bf16)
        out[...] = dot(rows, pick_t).astype(bf16)


def coupling_body(coupling, order, row_dof, out, out_t):
    pick_t = jnp.where(iota((NI, NI), 0) == row_dof[...], 1.0, 0.0).astype(bf16)
    ranked = jnp.dot(order[...], coupling[...], precision=highest, preferred_element_type=f32)
    hi, lo = split(ranked)
    hi, lo = dot(hi, pick_t), dot(lo, pick_t)
    out[...] = jnp.concatenate([hi, lo], 0).astype(bf16)
    tall = jnp.concatenate([hi, hi, lo, jnp.zeros_like(lo)], 0)
    out_t[...] = tall.T.astype(bf16)


def neighbours(stride, pivot):
    left = pivot - stride if pivot - stride >= 0 else None
    right = pivot + stride if pivot + stride < BLOCKS else None
    return left, right


def coarse_body(rows, columns, x, factor, diag, side):
    lane8 = iota((8, 128), 1)
    sub8 = iota((8, 128), 0)
    r0, c0 = iota((128, 128), 0), iota((128, 128), 1)
    r72, c72 = iota((72, 128), 0), iota((72, 128), 1)
    start = jnp.where((r0 == c0) & (r0 % 8 >= 6) & (r0 < 72), 1.0, 0.0)
    for j in range(BLOCKS):
        diag[j] = start
        side[j] = jnp.zeros((128, 256), f32)

    def piece(tile, right_a, lower_a, right_b, r):
        offset = (right_a * 2 + lower_a) * 32 + right_b * 16
        moved = pltpu.roll(tile, (r * 8 - offset) % 128, 1)
        return jnp.where((lane8 >= r * 8) & (lane8 < r * 8 + 16), moved, 0.0)

    def gather(pair, _):
        for odd in (0, 1):
            c = pair * 2 + odd
            tiles = [x[pl.ds(pl.multiple_of((r * columns + c) * 8, 8), 8), :] for r in range(rows)]
            for right in (0, 1):
                for i in range(rows + 1):
                    acc = diag[c + right, i * 8 : i * 8 + 8, :]
                    for lower in (0, 1):
                        if 0 <= i - lower < rows:
                            acc = acc + piece(tiles[i - lower], right, lower, right, i - lower)
                    diag[c + right, i * 8 : i * 8 + 8, :] = acc
            right_a = 0 if odd else 1
            at = 128 if odd else 0
            for i in range(rows + 1):
                acc = jnp.zeros((8, 128), f32)
                for lower in (0, 1):
                    if 0 <= i - lower < rows:
                        acc = acc + piece(tiles[i - lower], right_a, lower, 1 - right_a, i - lower)
                side[pair * 2 + 1, i * 8 : i * 8 + 8, at : at + 128] = acc
        return 0

    lax.fori_loop(0, columns // 2, gather, 0)

    def invert(blocks):
        def eliminate(own, own_turned, inside, i):
            pivot = {
                (p, q): jnp.broadcast_to(own_turned[p : p + 1, q : q + 1], (8, 128))
                for p in range(6)
                for q in range(p, 6)
            }
            line = [
                jnp.where(
                    inside,
                    jnp.where(lane8 - i * 8 == p, 1.0, 0.0),
                    jnp.broadcast_to(own[p : p + 1, :], (8, 128)),
                )
                for p in range(6)
            ]
            for p in range(6):
                inverse = 1.0 / pivot[p, p]
                scaled = {q: pivot[p, q] * inverse for q in range(p + 1, 6)}
                line[p] = line[p] * inverse
                for q in range(6):
                    if q < p:
                        line[q] = line[q] - pivot[q, p] * line[p]
                        for c in range(p + 1, 6):
                            pivot[q, c] = pivot[q, c] - pivot[q, p] * scaled[c]
                    if q > p:
                        line[q] = line[q] - pivot[p, q] * line[p]
                        for c in range(q, 6):
                            pivot[q, c] = pivot[q, c] - pivot[p, q] * scaled[c]
                for q in range(p + 1, 6):
                    pivot[p, q] = scaled[q]
            return line

        def vertex(i, _):
            inside = (lane8 >= i * 8) & (lane8 < i * 8 + 8)
            base = pl.multiple_of(i * 8, 8)
            own = [diag[j, pl.ds(base, 8), :] for j in blocks]
            own_turned = [pltpu.roll(t, 128 - i * 8, 1) for t in own]
            lines = [eliminate(own[n], own_turned[n], inside, i) for n in range(len(blocks))]
            for n, j in enumerate(blocks):
                wide = own[n]
                for p in range(6):
                    wide = jnp.where(sub8 == p, lines[n][p], wide)
                whole = diag[j, 0:72, :]
                turned = pltpu.roll(whole, 128 - i * 8, 1)[:, :8]
                acc = jnp.where((c72 >= i * 8) & (c72 < i * 8 + 8), 0.0, whole) - jnp.dot(
                    turned, jnp.where(sub8 < 6, wide, 0.0), precision=highest, preferred_element_type=f32
                )
                diag[j, 0:72, :] = jnp.where(
                    (r72 >= i * 8) & (r72 < i * 8 + 8), jnp.concatenate([wide] * 9, 0), acc
                )
            return 0

        lax.fori_loop(0, 9, vertex, 0)

    for level, (stride, pivots) in enumerate(LEVELS):
        invert(pivots)
        later = LEVELS[level + 1][1] if level + 1 < len(LEVELS) else ()
        for p in pivots:
            left, right = neighbours(stride, p)
            coupled = side[p]
            gain = jnp.dot(diag[p], coupled, precision=highest, preferred_element_type=f32)
            hi, lo = split(gain)
            factor[p, :, 256:] = jnp.concatenate([hi, lo], 1)
            schur = jnp.dot(coupled.T, gain, precision=highest, preferred_element_type=f32)
            if left is not None:
                diag[left] = diag[left] - schur[:128, :128]
            if right is not None:
                diag[right] = diag[right] - schur[128:, 128:]
            if left is not None and right is not None:
                if left in later:
                    side[left, :, 128:] = -schur[:128, 128:]
                else:
                    side[right, :, :128] = -schur[128:, :128]
    invert((ROOT,))
    factor[ROOT, :, 256:] = jnp.zeros((128, 512), bf16)
    for j in range(BLOCKS):
        hi, lo = split(diag[j])
        factor[j, :, :256] = jnp.concatenate([hi, lo], 1)


def coarse_factor(blocks, rows, columns):
    return call(
        functools.partial(coarse_body, rows, columns),
        (blocks,),
        [((BLOCKS, 128, 768), bf16)],
        [
            pltpu.VMEM((BLOCKS, 128, 128), f32),
            pltpu.VMEM((BLOCKS, 128, 256), f32),
        ],
        us=35.0,
        mib=12,
    )[0]


def row_times(x, hi, lo, transposed=False):
    high = x.astype(bf16).astype(f32)
    both = jnp.concatenate([high, x - high], 0).astype(bf16)
    dims = (((1,), (1 if transposed else 0,)), ((), ()))
    out = lax.dot_general(both, hi, dims, preferred_element_type=f32)
    out = out + lax.dot_general(both, lo, dims, preferred_element_type=f32)
    return out[:8] + out[8:]


def coarse_solve(rows, columns, w, factor, placed, solved):
    lane16 = iota((16, 128), 1)
    placed[...] = jnp.zeros_like(placed)
    solved[...] = jnp.zeros_like(solved)
    for k in range(4):
        for right in (0, 1):
            offset = k * 32 + right * 16
            acc = jnp.zeros((16, 128), f32)
            for r in range(rows):
                moved = pltpu.roll(w[r * columns : (r + 1) * columns, :], (r * 8 - offset) % 128, 1)
                take = (lane16 >= r * 8) & (lane16 < r * 8 + 16) & (lane16 % 8 < 6)
                acc = acc + jnp.where(take, moved, 0.0)
            at = k * 24 + 1 + right
            placed[at : at + 16, :] = placed[at : at + 16, :] + acc
    b = [placed[pl.ds(j + 1, 8, stride=24), :] for j in range(BLOCKS)]
    none = jnp.zeros((8, 128), f32)
    y, sol = [none] * BLOCKS, [none] * BLOCKS
    for stride, pivots in LEVELS:
        for p in pivots:
            left, right = neighbours(stride, p)
            gb = row_times(b[p], factor[p, :, 256:512], factor[p, :, 512:])
            if left is not None:
                b[left] = b[left] - gb[:, :128]
            if right is not None:
                b[right] = b[right] - gb[:, 128:]
            y[p] = row_times(b[p], factor[p, :, :128], factor[p, :, 128:256])
    sol[ROOT] = row_times(b[ROOT], factor[ROOT, :, :128], factor[ROOT, :, 128:256])
    for stride, pivots in LEVELS[::-1]:
        for p in pivots:
            left, right = neighbours(stride, p)
            pair = jnp.concatenate(
                [none if left is None else sol[left], none if right is None else sol[right]], 1
            )
            sol[p] = y[p] - row_times(pair, factor[p, :, 256:512], factor[p, :, 512:], True)
    for j in range(BLOCKS):
        solved[pl.ds(j + 1, 8, stride=24), :] = sol[j]
    product = placed[...] * solved[...]
    energy = [jnp.sum(product[k * 24 : k * 24 + 24, :], keepdims=True) for k in range(4)]
    answers = []
    for r in range(rows):
        own, beside, beyond = (jnp.zeros((16, 128), f32) for _ in range(3))

        def place(acc, k, column, source, offset, size):
            at = k * 24 + 1 + column
            moved = pltpu.roll(solved[at : at + 16, :], (offset - source * 8) % 128, 1)
            return acc + jnp.where((lane16 >= offset) & (lane16 < offset + size), moved, 0.0)

        for k in range(4):
            for right in (0, 1):
                own = place(own, k, right, r, k * 32 + right * 16, 16)
                beside = place(beside, k, (2, -1)[right], r, k * 32 + right * 16, 16)
                beyond = place(beyond, k, right, r + 2, k * 32 + right * 8, 8)
                if r > 0:
                    beyond = place(beyond, k, right, r - 1, k * 32 + 16 + right * 8, 8)
        answers.append((own, beside, beyond))
    return answers, energy


def lane_sum(total, at):
    lane = iota((1, 128), 1)
    return jnp.sum(jnp.where(lane == at, total, 0.0), axis=1, keepdims=True)


def by_case(values):
    lane = iota((1, 128), 1)
    out = jnp.zeros((1, 128), f32)
    for k in range(4):
        out = jnp.where(lane // 32 == k, values[k], out)
    return out


def write_answers(out, answers, columns, first, second):
    lane = iota((1, 128), 1)
    for r, (acc, beside, beyond) in enumerate(answers):
        acc = jnp.where(lane % 32 == 6, first, acc)
        acc = jnp.where(lane % 32 == 7, second, acc)
        out[r * columns : (r + 1) * columns, :] = jnp.concatenate([acc, beside, beyond], 1)


def first_solve_body(rows, columns, w, factor, out, state, placed, solved):
    answers, energy = coarse_solve(rows, columns, w, factor, placed, solved)
    total = jnp.sum(w[...], axis=0, keepdims=True)
    dots = by_case([lane_sum(total, k * 32 + 6) for k in range(4)])
    curvature = by_case([lane_sum(total, k * 32 + 7) + energy[k] for k in range(4)])
    state[...] = jnp.concatenate([dots, curvature, jnp.zeros((6, 128), f32)], 0)
    step = dots / curvature
    write_answers(out, answers, columns, step, step)


def second_solve_body(rows, columns, w, state, factor, out, placed, solved):
    answers, energy = coarse_solve(rows, columns, w, factor, placed, solved)
    total = jnp.sum(w[...], axis=0, keepdims=True)
    dots = by_case([lane_sum(total, k * 32 + 6) for k in range(4)])
    own = by_case([lane_sum(total, k * 32 + 7) + energy[k] for k in range(4)])
    cross = by_case([lane_sum(total, k * 32 + 14) for k in range(4)])
    ratio = dots / state[0:1, :]
    curvature = own + ratio * (2.0 * cross + ratio * state[1:2, :])
    write_answers(out, answers, columns, dots / curvature, ratio)


def solve_scratch():
    return [pltpu.VMEM((192, 128), f32), pltpu.VMEM((192, 128), f32)]


def mask_of(counts, k):
    return iota((CAP, R), 0) < counts[k]


def product(hi, lo, x, k):
    a, b = hi[k * CAP : (k + 1) * CAP, :], lo[k * CAP : (k + 1) * CAP, :]
    xh, xl = x
    return dot(a, xh) + dot(a, xl) + dot(b, xh)


def start_body(counts, rhs, west, north, hi, lo, coupling, r4, *t):
    for k, (values, sign) in enumerate(((rhs[0], 1.0), (rhs[1], 1.0), (west[:CAP, :], -1.0), (north[:CAP, :], -1.0))):
        r4[k * CAP : (k + 1) * CAP, :] = jnp.where(mask_of(counts, k), values * sign, 0.0)
    x = split(r4[...])
    rows = coupling[:32, :].astype(f32) + coupling[32:, :].astype(f32)
    for k in range(4):
        t[k][:CAP, :] = product(hi, lo, x, k)
        own = rows[:, k * CAP : (k + 1) * CAP]
        t[k][CAP:, :] = jnp.concatenate([own[:16, :], own[16:, :]], 1)


def joined_body(own_t, e0, e1, e2, e3, out):
    other = jnp.concatenate(
        [jnp.concatenate([e[CAP:, :CAP], e[CAP:, CAP:]], 0) for e in (e0, e1, e2, e3)], 1
    )
    hi = other.astype(bf16).astype(f32)
    lo = other - hi
    tall = jnp.concatenate([hi, hi, lo, jnp.zeros_like(lo)], 0)
    out[:, :128] = own_t[...]
    out[:, 128:] = (-tall.T).astype(bf16)


def jumped(counts, t, received, k):
    return jnp.where(mask_of(counts, k), t[k][:CAP, :] - received[k][:CAP, :], 0.0)


def payload(loads, rows_of_dots):
    sub = iota((32, R), 0)
    for at, values in rows_of_dots:
        loads = jnp.where(sub == at, values, loads)
    tall = jnp.concatenate([loads[:, k * 128 : (k + 1) * 128] for k in range(4)], 0)
    return tall.T


def corner_loads(coupling, x):
    xh, xl = x
    both = dot(coupling[...], xh)
    return both[:32] + both[32:] + dot(coupling[:32, :], xl)


def sum_rows(x):
    return jnp.sum(x, axis=0, keepdims=True)


def operate(counts, t, received, hi, lo, coupling, field, u):
    for k in range(4):
        field[k * CAP : (k + 1) * CAP, :] = jumped(counts, t, received, k)
    x = split(field[...])
    loads = corner_loads(coupling, x)
    energy = jnp.zeros((1, R), f32)
    for k in range(4):
        part = product(hi, lo, x, k)
        u[k][...] = part
        energy = energy + sum_rows(part * field[k * CAP : (k + 1) * CAP, :])
    return loads, energy


def first_operator_body(
    counts, t0, t1, t2, t3, e0, e1, e2, e3, r4, hi, lo, coupling, z4, out, *u
):
    loads, energy = operate(counts, (t0, t1, t2, t3), (e0, e1, e2, e3), hi, lo, coupling, z4, u)
    dots = sum_rows(r4[: 2 * CAP, :] * z4[: 2 * CAP, :])
    out[...] = payload(loads, ((6, dots), (7, energy)))


def second_operator_body(
    counts, t0, t1, t2, t3, e0, e1, e2, e3, r1, w4, hi, lo, coupling, z4, out, *u
):
    loads, energy = operate(counts, (t0, t1, t2, t3), (e0, e1, e2, e3), hi, lo, coupling, z4, u)
    owned = z4[: 2 * CAP, :]
    dots = sum_rows(r1[...] * owned)
    cross = sum_rows(w4[...] * owned)
    out[...] = payload(loads, ((6, dots), (7, energy), (14, cross)))


def unpack(answer):
    flat = []
    for group in range(3):
        tall = answer[:, group * 128 : (group + 1) * 128].T
        flat.append(jnp.concatenate([tall[k * 32 : (k + 1) * 32, :] for k in range(4)], 1))
    scalars = flat[0][0:8, :]
    keep = iota((32, R), 0) % 8 < 6
    own, beside, beyond = (jnp.where(keep, x, 0.0) for x in flat)
    o = [own[v * 8 : v * 8 + 8, :] for v in range(4)]
    b = [beyond[v * 8 : v * 8 + 8, :] for v in range(4)]
    others = (
        jnp.concatenate([own[16:, :], beside[:16, :]], 0),
        jnp.concatenate([o[1], b[0], o[3], b[1]], 0),
        jnp.concatenate([beside[16:, :], own[:16, :]], 0),
        jnp.concatenate([b[2], o[0], b[3], o[2]], 0),
    )

    def parts(x):
        hi = x.astype(bf16).astype(f32)
        return [hi, x - hi, hi, jnp.zeros_like(hi)]

    mine = parts(own)
    return scalars, [jnp.concatenate(mine + parts(x), 0).astype(bf16) for x in others]


def image_of(counts, u, received, joined, sides, k):
    across = dot(joined[k * CAP : (k + 1) * CAP, :], sides[k])
    return jnp.where(mask_of(counts, k), u[k][...] - received[k][...] + across, 0.0)


def precondition_body(
    counts, u0, u1, u2, u3, e0, e1, e2, e3, answer, joined, r4, hi, lo,
    r1, w, scalars, s0, s1, s2, s3, work,
):
    u, received = (u0, u1, u2, u3), (e0, e1, e2, e3)
    first, sides = unpack(answer)
    scalars[...] = first
    step = first[6:7, :]
    for k in range(4):
        rows = slice(k * CAP, (k + 1) * CAP)
        image = image_of(counts, u, received, joined, sides, k)
        work[rows, :] = r4[rows, :] - step * image
        if k < 2:
            w[rows, :] = image
            r1[rows, :] = work[rows, :]
    x = split(work[...])
    for k, out in enumerate((s0, s1, s2, s3)):
        out[...] = product(hi, lo, x, k)


def end_body(counts, u0, u1, e0, e1, answer, joined, z4, z1, r1, w, first, mult, residual):
    u, received = (u0, u1), (e0, e1)
    second, sides = unpack(answer)
    step, last, ratio = first[6:7, :], second[6:7, :], second[7:8, :]
    for k in range(2):
        rows = slice(k * CAP, (k + 1) * CAP)
        start = z4[rows, :]
        mult[k] = step * start + last * (z1[rows, :] + ratio * start)
        image = image_of(counts, u, received, joined, sides, k) + ratio * w[rows, :]
        residual[k] = r1[rows, :] - last * image


def shift(block, axis, distance):
    devices = range(lax.axis_size(axis))
    route = [(i - distance, i) for i in devices if i - distance in devices]
    return lax.ppermute(block, axis, route)


def exchange(t):
    return (
        shift(t[2], "sy", -1),
        shift(t[3], "sx", -1),
        shift(t[0], "sy", 1),
        shift(t[1], "sx", 1),
    )


def everywhere(blocks):
    return lax.all_to_all(blocks, BOTH, 0, 0, tiled=True)


def vertex_order(corner_map, rhs):
    names = corner_map[0]
    tags = names[None] + 1
    tail = jnp.pad(tags.astype(f32), ((0, 7), (0, R - tags.shape[1])))
    east, south = shift(tags, "sy", -1)[0], shift(tags, "sx", -1)[0]
    from_west = shift(jnp.concatenate([rhs[0], tail], 0), "sy", 1)
    from_north = shift(jnp.concatenate([rhs[1], tail], 0), "sx", 1)
    west, north = (x[CAP, : tags.shape[1]].astype(jnp.int32) for x in (from_west, from_north))

    def named(other):
        return jnp.any(tags[0][:, None] == other[None, :], axis=1)

    last_column = lax.axis_index("sy") == lax.axis_size("sy") - 1
    last_row = lax.axis_index("sx") == lax.axis_size("sx") - 1
    right = jnp.where(last_column, ~named(west), named(east)).astype(jnp.int32)
    lower = jnp.where(last_row, ~named(north), named(south)).astype(jnp.int32)
    vertex = right * 2 + lower
    before = (vertex[:, None] == vertex[None, :]) & (names[None, :] < names[:, None])
    row = vertex * 8 + jnp.sum(before.astype(jnp.int32), axis=1)
    order = (jnp.arange(32, dtype=jnp.int32)[:, None] == row[None, :]).astype(f32)
    return order, from_west, from_north


def on_device(
    jump_rhs, counts, slot_dof, remainder_inv, schur_matrix, coupling, coarse_local, corner_map
):
    rows, columns = lax.axis_size("sx"), lax.axis_size("sy")
    devices = rows * columns
    counts = counts[0]
    rhs = jump_rhs[0]
    order, west, north = vertex_order(corner_map, rhs)
    local = jnp.dot(jnp.dot(order, coarse_local[0], precision=highest), order.T, precision=highest)
    local = jnp.concatenate([local[v * 8 : v * 8 + 8] for v in range(4)], 1)
    blocks = everywhere(jnp.broadcast_to(local[None], (devices, 8, 128)))

    row_dof, col_dof = slot_dof, slot_dof.reshape(NI, 1)
    matrix_outs = [((NI, NI), bf16), ((NI, NI), bf16)]
    sh, sl = call(permute_body, (schur_matrix[0], row_dof, col_dof), matrix_outs, us=12.0, mib=32)
    cpl, cpl_t = call(
        coupling_body, (coupling[0], order, row_dof), [((64, NI), bf16), ((NI, 128), bf16)], us=1.5, mib=12
    )
    rh, rl = call(permute_body, (remainder_inv[0], row_dof, col_dof), matrix_outs, us=12.0, mib=32)
    factor = coarse_factor(blocks.reshape(devices * 8, 128), rows, columns)

    field, half, slab = ((NI, R), f32), ((2 * CAP, R), f32), ((CAP, R), f32)
    longer = ((CAP + 16, R), f32)
    message, wide, few = ((128, 128), f32), ((128, 384), f32), ((8, R), f32)
    specs = lambda n: [SM] + [VM] * n

    r4, *t = call(
        start_body, (counts, rhs, west, north, sh, sl, cpl), [field] + [longer] * 4, (), specs(6), 7.0
    )
    received = exchange(t)
    (joined,) = call(joined_body, (cpl_t, *received), [((NI, 256), bf16)], us=1.0, mib=12)
    z4, out, *u = call(
        first_operator_body,
        (counts, *t, *received, r4, rh, rl, cpl),
        [field, message] + [slab] * 4,
        (),
        specs(12),
        8.0,
    )
    arrived = everywhere(out)
    received = exchange(u)
    answer, state = call(
        functools.partial(first_solve_body, rows, columns),
        (arrived, factor),
        [wide, ((8, 128), f32)],
        solve_scratch(),
        us=2.5,
        mib=8,
    )
    r1, w, first, *t = call(
        precondition_body,
        (counts, *u, *received, everywhere(answer), joined, r4, sh, sl),
        [half, half, few] + [slab] * 4,
        [pltpu.VMEM((NI, R), f32)],
        specs(13),
        8.0,
    )
    received = exchange(t)
    z1, out, *u = call(
        second_operator_body,
        (counts, *t, *received, r1, w, rh, rl, cpl),
        [field, message] + [slab] * 4,
        (),
        specs(13),
        8.0,
    )
    arrived = everywhere(out)
    received = shift(u[2], "sy", -1), shift(u[3], "sx", -1)
    (answer,) = call(
        functools.partial(second_solve_body, rows, columns),
        (arrived, state, factor),
        [wide],
        solve_scratch(),
        us=2.5,
        mib=8,
    )
    own = ((2, CAP, R), f32)
    multipliers, residual = call(
        end_body,
        (counts, u[0], u[1], *received, everywhere(answer), joined, z4, z1, r1, w, first),
        [own, own],
        (),
        specs(11),
        4.0,
    )
    return multipliers[None], residual[None]


def solution(mesh):
    four, three, two = P(BOTH, None, None, None), P(BOTH, None, None), P(BOTH, None)
    return jax.shard_map(
        on_device,
        mesh=mesh,
        in_specs=(four, two, two, three, three, three, three, two),
        out_specs=(four, four),
        check_vma=False,
    )
```

```python
import functools

import jax
import jax.numpy as jnp
from jax import lax
from jax.experimental import pallas as pl
from jax.experimental.pallas import tpu as pltpu
from jax.sharding import PartitionSpec as P

f32, bf16 = jnp.float32, jnp.bfloat16
highest = lax.Precision.HIGHEST
BOTH = ("sx", "sy")
CAP, R, NI = 256, 512, 1024
LEVELS = (
    (1, tuple(range(1, 16, 2))),
    (2, (2, 6, 10, 14)),
    (4, (4, 12)),
    (8, (0, 16)),
)
ROOT = 8
BLOCKS = 17
VM = pl.BlockSpec(memory_space=pltpu.VMEM)
SM = pl.BlockSpec(memory_space=pltpu.SMEM)
HB = pl.BlockSpec(memory_space=pltpu.HBM)


def call(body, ins, outs, scratch=(), specs=None, us=1.0, mib=24, far=(), out=()):
    return pl.pallas_call(
        body,
        out_shape=[
            pltpu.HBM(s, d) if n in far + out else jax.ShapeDtypeStruct(s, d) for n, (s, d) in enumerate(outs)
        ],
        in_specs=specs if specs is not None else [VM] * len(ins),
        out_specs=[HB if n in far else VM for n in range(len(outs))],
        scratch_shapes=list(scratch),
        cost_estimate=pl.CostEstimate(flops=int(us * 1.15e9), bytes_accessed=int(us * 1e6), transcendentals=0),
        compiler_params=pltpu.CompilerParams(vmem_limit_bytes=mib * 1024 * 1024),
    )(*[
        pltpu.with_memory_space_constraint(x, pltpu.HBM) if specs is not None and specs[n] is HB else x
        for n, x in enumerate(ins)
    ])


def dot(a, b):
    return jnp.dot(a, b, preferred_element_type=f32)


def split(x):
    hi = x.astype(bf16)
    return hi, (x - hi.astype(f32)).astype(bf16)


def iota(shape, axis):
    return lax.broadcasted_iota(jnp.int32, shape, axis)


MATRIX_SCRATCH = [
    pltpu.VMEM((NI, NI), bf16),
    pltpu.VMEM((NI, NI), bf16),
    pltpu.SemaphoreType.DMA((8,)),
]


def slab_copies(sources, targets, sems):
    return [
        [
            pltpu.make_async_copy(
                source.at[k * CAP : (k + 1) * CAP, :], target.at[k * CAP : (k + 1) * CAP, :], sems.at[k * 2 + n]
            )
            for n, (source, target) in enumerate(zip(sources, targets))
        ]
        for k in range(4)
    ]


class Matrix:
    def __init__(self, hi, lo, hi_here, lo_here, sems):
        self.here = hi_here, lo_here
        self.copies = slab_copies((hi, lo), self.here, sems)
        for pair in self.copies:
            for copy in pair:
                copy.start()

    def times(self, x, k):
        for copy in self.copies[k]:
            copy.wait()
        a, b = (part[k * CAP : (k + 1) * CAP, :] for part in self.here)
        xh, xl = x
        return dot(a, xh) + dot(a, xl) + dot(b, xh)


def permute_body(mat, row_dof, col_dof, hi_out, lo_out, hi_here, lo_here, sems):
    pick_t = jnp.where(iota((NI, NI), 0) == row_dof[...], 1.0, 0.0).astype(bf16)
    parts = split(mat[...])
    copies = slab_copies((hi_here, lo_here), (hi_out, lo_out), sems)
    for k in range(4):
        rows = slice(k * CAP, (k + 1) * CAP)
        pick = jnp.where(iota((CAP, NI), 1) == col_dof[rows, :], 1.0, 0.0).astype(bf16)
        for n, here in enumerate((hi_here, lo_here)):
            here[rows, :] = dot(dot(pick, parts[n]).astype(bf16), pick_t).astype(bf16)
            copies[k][n].start()
    for pair in copies:
        for copy in pair:
            copy.wait()


def coupling_body(coupling, order, row_dof, out, out_t):
    pick_t = jnp.where(iota((NI, NI), 0) == row_dof[...], 1.0, 0.0).astype(bf16)
    ranked = jnp.dot(order[...], coupling[...], precision=highest, preferred_element_type=f32)
    hi, lo = split(ranked)
    hi, lo = dot(hi, pick_t), dot(lo, pick_t)
    out[...] = jnp.concatenate([hi, lo], 0).astype(bf16)
    tall = jnp.concatenate([hi, hi, lo, jnp.zeros_like(lo)], 0)
    out_t[...] = tall.T.astype(bf16)


def neighbours(stride, pivot):
    left = pivot - stride if pivot - stride >= 0 else None
    right = pivot + stride if pivot + stride < BLOCKS else None
    return left, right


def coarse_body(rows, columns, x, factor, diag, side):
    lane8 = iota((8, 128), 1)
    sub8 = iota((8, 128), 0)
    r0, c0 = iota((128, 128), 0), iota((128, 128), 1)
    c72 = iota((72, 128), 1)
    start = jnp.where((r0 == c0) & (r0 % 8 >= 6) & (r0 < 72), 1.0, 0.0)
    for j in range(BLOCKS):
        diag[j] = start
        side[j] = jnp.zeros((128, 256), f32)

    def piece(tile, right_a, lower_a, right_b, r):
        offset = (right_a * 2 + lower_a) * 32 + right_b * 16
        moved = pltpu.roll(tile, (r * 8 - offset) % 128, 1)
        return jnp.where((lane8 >= r * 8) & (lane8 < r * 8 + 16), moved, 0.0)

    def gather(pair, _):
        for odd in (0, 1):
            c = pair * 2 + odd
            tiles = [x[pl.ds(pl.multiple_of((r * columns + c) * 8, 8), 8), :] for r in range(rows)]
            for right in (0, 1):
                for i in range(rows + 1):
                    acc = diag[c + right, i * 8 : i * 8 + 8, :]
                    for lower in (0, 1):
                        if 0 <= i - lower < rows:
                            acc = acc + piece(tiles[i - lower], right, lower, right, i - lower)
                    diag[c + right, i * 8 : i * 8 + 8, :] = acc
            right_a = 0 if odd else 1
            at = 128 if odd else 0
            for i in range(rows + 1):
                acc = jnp.zeros((8, 128), f32)
                for lower in (0, 1):
                    if 0 <= i - lower < rows:
                        acc = acc + piece(tiles[i - lower], right_a, lower, 1 - right_a, i - lower)
                side[pair * 2 + 1, i * 8 : i * 8 + 8, at : at + 128] = acc
        return 0

    lax.fori_loop(0, columns // 2, gather, 0)

    def invert(blocks):
        def eliminate(own, own_turned, inside, i):
            pivot = {
                (p, q): jnp.broadcast_to(own_turned[p : p + 1, q : q + 1], (8, 128))
                for p in range(6)
                for q in range(p, 6)
            }
            line = [
                jnp.where(
                    inside,
                    jnp.where(lane8 - i * 8 == p, 1.0, 0.0),
                    jnp.broadcast_to(own[p : p + 1, :], (8, 128)),
                )
                for p in range(6)
            ]
            for p in range(6):
                inverse = 1.0 / pivot[p, p]
                scaled = {q: pivot[p, q] * inverse for q in range(p + 1, 6)}
                line[p] = line[p] * inverse
                for q in range(6):
                    if q < p:
                        line[q] = line[q] - pivot[q, p] * line[p]
                        for c in range(p + 1, 6):
                            pivot[q, c] = pivot[q, c] - pivot[q, p] * scaled[c]
                    if q > p:
                        line[q] = line[q] - pivot[p, q] * line[p]
                        for c in range(q, 6):
                            pivot[q, c] = pivot[q, c] - pivot[p, q] * scaled[c]
                for q in range(p + 1, 6):
                    pivot[p, q] = scaled[q]
            return line

        table = [diag[j, 0:72, :] for j in blocks]
        own = [t[0:8, :] for t in table]
        for i in range(9):
            low, high = i * 8, i * 8 + 8
            inside = (lane8 >= low) & (lane8 < high)
            ahead = []
            for n, t in enumerate(table):
                line = eliminate(own[n], own[n][:, low:high], inside, i)
                wide = own[n]
                for p in range(6):
                    wide = jnp.where(sub8 == p, line[p], wide)
                next_own = None
                if i < 8:
                    next_old = t[high : high + 8, :]
                    next_own = jnp.where(inside, 0.0, next_old)
                    for p in range(6):
                        next_own = next_own - next_old[:, low + p : low + p + 1] * line[p]
                ahead.append(next_own)
                moved = jnp.dot(
                    t[:, low:high],
                    jnp.where(sub8 < 6, wide, 0.0),
                    precision=highest,
                    preferred_element_type=f32,
                )
                kept = jnp.where((c72 >= low) & (c72 < high), 0.0, t) - moved
                tiles = [kept[:low, :]] if i else []
                tiles.append(wide)
                if i < 8:
                    tiles.append(next_own)
                if i < 7:
                    tiles.append(kept[high + 8 :, :])
                table[n] = jnp.concatenate(tiles, 0)
            own = ahead
        for n, j in enumerate(blocks):
            diag[j, 0:72, :] = table[n]

    for level, (stride, pivots) in enumerate(LEVELS):
        invert(pivots)
        later = LEVELS[level + 1][1] if level + 1 < len(LEVELS) else ()
        for p in pivots:
            left, right = neighbours(stride, p)
            coupled = side[p]
            gain = jnp.dot(diag[p], coupled, precision=highest, preferred_element_type=f32)
            hi, lo = split(gain)
            factor[p, :, 256:] = jnp.concatenate([hi, lo], 1)
            schur = jnp.dot(coupled.T, gain, precision=highest, preferred_element_type=f32)
            if left is not None:
                diag[left] = diag[left] - schur[:128, :128]
            if right is not None:
                diag[right] = diag[right] - schur[128:, 128:]
            if left is not None and right is not None:
                if left in later:
                    side[left, :, 128:] = -schur[:128, 128:]
                else:
                    side[right, :, :128] = -schur[128:, :128]
    invert((ROOT,))
    factor[ROOT, :, 256:] = jnp.zeros((128, 512), bf16)
    for j in range(BLOCKS):
        hi, lo = split(diag[j])
        factor[j, :, :256] = jnp.concatenate([hi, lo], 1)


def row_times(x, hi, lo, transposed=False):
    high = x.astype(bf16).astype(f32)
    both = jnp.concatenate([high, x - high], 0).astype(bf16)
    dims = (((1,), (1 if transposed else 0,)), ((), ()))
    out = lax.dot_general(both, hi, dims, preferred_element_type=f32)
    out = out + lax.dot_general(both, lo, dims, preferred_element_type=f32)
    return out[:8] + out[8:]


def coarse_solve(rows, columns, w, factor, placed, solved, pending=None):
    lane16 = iota((16, 128), 1)
    placed[...] = jnp.zeros_like(placed)
    solved[...] = jnp.zeros_like(solved)
    for k in range(4):
        for right in (0, 1):
            offset = k * 32 + right * 16
            acc = jnp.zeros((16, 128), f32)
            for r in range(rows):
                moved = pltpu.roll(w[r * columns : (r + 1) * columns, :], (r * 8 - offset) % 128, 1)
                take = (lane16 >= r * 8) & (lane16 < r * 8 + 16) & (lane16 % 8 < 6)
                acc = acc + jnp.where(take, moved, 0.0)
            at = k * 24 + 1 + right
            placed[at : at + 16, :] = placed[at : at + 16, :] + acc
    b = [placed[pl.ds(j + 1, 8, stride=24), :] for j in range(BLOCKS)]
    if pending is not None:
        pending.wait()
    none = jnp.zeros((8, 128), f32)
    y, sol = [none] * BLOCKS, [none] * BLOCKS
    for stride, pivots in LEVELS:
        for p in pivots:
            left, right = neighbours(stride, p)
            gb = row_times(b[p], factor[p, :, 256:512], factor[p, :, 512:])
            if left is not None:
                b[left] = b[left] - gb[:, :128]
            if right is not None:
                b[right] = b[right] - gb[:, 128:]
            y[p] = row_times(b[p], factor[p, :, :128], factor[p, :, 128:256])
    sol[ROOT] = row_times(b[ROOT], factor[ROOT, :, :128], factor[ROOT, :, 128:256])
    for stride, pivots in LEVELS[::-1]:
        for p in pivots:
            left, right = neighbours(stride, p)
            pair = jnp.concatenate(
                [none if left is None else sol[left], none if right is None else sol[right]], 1
            )
            sol[p] = y[p] - row_times(pair, factor[p, :, 256:512], factor[p, :, 512:], True)
    for j in range(BLOCKS):
        solved[pl.ds(j + 1, 8, stride=24), :] = sol[j]
    product = placed[...] * solved[...]
    energy = [jnp.sum(product[k * 24 : k * 24 + 24, :], keepdims=True) for k in range(4)]
    answers = []
    for r in range(rows):
        own, beside, beyond = (jnp.zeros((16, 128), f32) for _ in range(3))

        def place(acc, k, column, source, offset, size):
            at = k * 24 + 1 + column
            moved = pltpu.roll(solved[at : at + 16, :], (offset - source * 8) % 128, 1)
            return acc + jnp.where((lane16 >= offset) & (lane16 < offset + size), moved, 0.0)

        for k in range(4):
            for right in (0, 1):
                own = place(own, k, right, r, k * 32 + right * 16, 16)
                beside = place(beside, k, (2, -1)[right], r, k * 32 + right * 16, 16)
                beyond = place(beyond, k, right, r + 2, k * 32 + right * 8, 8)
                if r > 0:
                    beyond = place(beyond, k, right, r - 1, k * 32 + 16 + right * 8, 8)
        answers.append((own, beside, beyond))
    return answers, energy


def lane_sum(total, at):
    lane = iota((1, 128), 1)
    return jnp.sum(jnp.where(lane == at, total, 0.0), axis=1, keepdims=True)


def by_case(values):
    lane = iota((1, 128), 1)
    out = jnp.zeros((1, 128), f32)
    for k in range(4):
        out = jnp.where(lane // 32 == k, values[k], out)
    return out


def write_answers(out, answers, columns, first, second):
    lane = iota((1, 128), 1)
    for r, (acc, beside, beyond) in enumerate(answers):
        acc = jnp.where(lane % 32 == 6, first, acc)
        acc = jnp.where(lane % 32 == 7, second, acc)
        for group, values in enumerate((acc, beside, beyond)):
            out[pl.ds(r * columns * 3 + group, 16, stride=3), :] = values


def first_solve_body(rows, columns, blocks, w, out, state, kept, factor, sem, placed, solved, diag, side):
    coarse_body(rows, columns, blocks, factor, diag, side)
    keep = pltpu.make_async_copy(factor, kept, sem)
    keep.start()
    answers, energy = coarse_solve(rows, columns, w, factor, placed, solved)
    total = jnp.sum(w[...], axis=0, keepdims=True)
    dots = by_case([lane_sum(total, k * 32 + 6) for k in range(4)])
    curvature = by_case([lane_sum(total, k * 32 + 7) + energy[k] for k in range(4)])
    state[...] = jnp.concatenate([dots, curvature, jnp.zeros((6, 128), f32)], 0)
    step = dots / curvature
    write_answers(out, answers, columns, step, step)
    keep.wait()


def second_solve_body(rows, columns, w, state, kept, out, factor, sem, placed, solved):
    bring = pltpu.make_async_copy(kept, factor, sem)
    bring.start()
    answers, energy = coarse_solve(rows, columns, w, factor, placed, solved, bring)
    total = jnp.sum(w[...], axis=0, keepdims=True)
    dots = by_case([lane_sum(total, k * 32 + 6) for k in range(4)])
    own = by_case([lane_sum(total, k * 32 + 7) + energy[k] for k in range(4)])
    cross = by_case([lane_sum(total, k * 32 + 14) for k in range(4)])
    ratio = dots / state[0:1, :]
    curvature = own + ratio * (2.0 * cross + ratio * state[1:2, :])
    write_answers(out, answers, columns, dots / curvature, ratio)


def solve_scratch():
    return [
        pltpu.VMEM((BLOCKS, 128, 768), bf16),
        pltpu.SemaphoreType.DMA,
        pltpu.VMEM((192, 128), f32),
        pltpu.VMEM((192, 128), f32),
    ]


def mask_of(counts, k):
    return iota((CAP, R), 0) < counts[k]


def residual_slots(counts, rhs, west, north, k):
    values = (rhs[0], rhs[1], None, None)[k] if k < 2 else -(west, north)[k - 2][:CAP, :]
    return jnp.where(mask_of(counts, k), values, 0.0)


def start_body(counts, rhs, west, north, hi, lo, coupling, t0, t1, t2, t3, *here):
    matrix = Matrix(hi, lo, *here)
    x = split(jnp.concatenate([residual_slots(counts, rhs, west, north, k) for k in range(4)], 0))
    rows = coupling[:32, :].astype(f32) + coupling[32:, :].astype(f32)
    for k, t in enumerate((t0, t1, t2, t3)):
        t[:CAP, :] = matrix.times(x, k)
        own = rows[:, k * CAP : (k + 1) * CAP]
        t[CAP:, :] = jnp.concatenate([own[:16, :], own[16:, :]], 1)


def joined_body(own_t, e0, e1, e2, e3, out):
    other = jnp.concatenate(
        [jnp.concatenate([e[CAP:, :CAP], e[CAP:, CAP:]], 0) for e in (e0, e1, e2, e3)], 1
    )
    hi = other.astype(bf16).astype(f32)
    lo = other - hi
    tall = jnp.concatenate([hi, hi, lo, jnp.zeros_like(lo)], 0)
    out[:, :128] = own_t[...]
    out[:, 128:] = (-tall.T).astype(bf16)


def jumped(counts, t, received, k):
    return jnp.where(mask_of(counts, k), t[k][:CAP, :] - received[k][:CAP, :], 0.0)


def payload(loads, rows_of_dots):
    sub = iota((32, R), 0)
    for at, values in rows_of_dots:
        loads = jnp.where(sub == at, values, loads)
    tall = jnp.concatenate([loads[:, k * 128 : (k + 1) * 128] for k in range(4)], 0)
    return tall.T


def corner_loads(coupling, x):
    xh, xl = x
    both = dot(coupling[...], xh)
    return both[:32] + both[32:] + dot(coupling[:32, :], xl)


def sum_rows(x):
    return jnp.sum(x, axis=0, keepdims=True)


def operate(counts, t, received, matrix, coupling, u):
    field = [jumped(counts, t, received, k) for k in range(4)]
    x = split(jnp.concatenate(field, 0))
    loads = corner_loads(coupling, x)
    energy = jnp.zeros((1, R), f32)
    for k in range(4):
        part = matrix.times(x, k)
        u[k][...] = part
        energy = energy + sum_rows(part * field[k])
    return field, loads, energy


def first_operator_body(
    counts, t0, t1, t2, t3, e0, e1, e2, e3, rhs, hi, lo, coupling,
    z, out, u0, u1, u2, u3, *here,
):
    matrix = Matrix(hi, lo, *here)
    u = (u0, u1, u2, u3)
    field, loads, energy = operate(counts, (t0, t1, t2, t3), (e0, e1, e2, e3), matrix, coupling, u)
    dots = jnp.zeros((1, R), f32)
    for k in range(2):
        z[k * CAP : (k + 1) * CAP, :] = field[k]
        dots = dots + sum_rows(rhs[k] * field[k])
    out[...] = payload(loads, ((6, dots), (7, energy)))


def second_operator_body(
    counts, t0, t1, t2, t3, e0, e1, e2, e3, r1, w4, hi, lo, coupling,
    z, out, u0, u1, u2, u3, *here,
):
    matrix = Matrix(hi, lo, *here)
    u = (u0, u1, u2, u3)
    field, loads, energy = operate(counts, (t0, t1, t2, t3), (e0, e1, e2, e3), matrix, coupling, u)
    dots, cross = jnp.zeros((1, R), f32), jnp.zeros((1, R), f32)
    for k in range(2):
        rows = slice(k * CAP, (k + 1) * CAP)
        z[rows, :] = field[k]
        dots = dots + sum_rows(r1[rows, :] * field[k])
        cross = cross + sum_rows(w4[rows, :] * field[k])
    out[...] = payload(loads, ((6, dots), (7, energy), (14, cross)))


def unpack(answer):
    flat = []
    for group in range(3):
        tall = answer[pl.ds(group, 128, stride=3), :].T
        flat.append(jnp.concatenate([tall[k * 32 : (k + 1) * 32, :] for k in range(4)], 1))
    scalars = flat[0][0:8, :]
    keep = iota((32, R), 0) % 8 < 6
    own, beside, beyond = (jnp.where(keep, x, 0.0) for x in flat)
    o = [own[v * 8 : v * 8 + 8, :] for v in range(4)]
    b = [beyond[v * 8 : v * 8 + 8, :] for v in range(4)]
    others = (
        jnp.concatenate([own[16:, :], beside[:16, :]], 0),
        jnp.concatenate([o[1], b[0], o[3], b[1]], 0),
        jnp.concatenate([beside[16:, :], own[:16, :]], 0),
        jnp.concatenate([b[2], o[0], b[3], o[2]], 0),
    )

    def parts(x):
        hi = x.astype(bf16).astype(f32)
        return [hi, x - hi, hi, jnp.zeros_like(hi)]

    mine = parts(own)
    return scalars, [jnp.concatenate(mine + parts(x), 0).astype(bf16) for x in others]


class Slabs:
    def __init__(self, sources, here, sems):
        self.here = here
        self.copies = [
            pltpu.make_async_copy(source, here.at[n], sems.at[n]) for n, source in enumerate(sources)
        ]
        for copy in self.copies:
            copy.start()

    def __getitem__(self, n):
        self.copies[n].wait()
        return self.here[n]


def slab_scratch(n):
    return [pltpu.VMEM((n, CAP, R), f32), pltpu.SemaphoreType.DMA((n,))]


def image_of(counts, slabs, joined, sides, k):
    across = dot(joined[k * CAP : (k + 1) * CAP, :], sides[k])
    return jnp.where(mask_of(counts, k), slabs[2 * k] - slabs[2 * k + 1] + across, 0.0)


def precondition_body(
    counts, u0, u1, u2, u3, e0, e1, e2, e3, answer, joined, rhs, west, north, hi, lo,
    r1, w, scalars, s0, s1, s2, s3, slab_here, slab_sems, *here,
):
    slabs = Slabs((u0, e0, u1, e1, u2, e2, u3, e3), slab_here, slab_sems)
    matrix = Matrix(hi, lo, *here)
    first, sides = unpack(answer)
    scalars[...] = first
    step = first[6:7, :]
    work = []
    for k in range(4):
        image = image_of(counts, slabs, joined, sides, k)
        work.append(residual_slots(counts, rhs, west, north, k) - step * image)
        if k < 2:
            w[k * CAP : (k + 1) * CAP, :] = image
            r1[k * CAP : (k + 1) * CAP, :] = work[k]
    x = split(jnp.concatenate(work, 0))
    for k, out in enumerate((s0, s1, s2, s3)):
        out[...] = matrix.times(x, k)


def end_body(counts, u0, u1, e0, e1, answer, joined, z4, z1, r1, w, first, mult, residual, *here):
    slabs = Slabs((u0, e0, u1, e1), *here)
    second, sides = unpack(answer)
    step, last, ratio = first[6:7, :], second[6:7, :], second[7:8, :]
    for k in range(2):
        rows = slice(k * CAP, (k + 1) * CAP)
        start = z4[rows, :]
        mult[k] = step * start + last * (z1[rows, :] + ratio * start)
        image = image_of(counts, slabs, joined, sides, k) + ratio * w[rows, :]
        residual[k] = r1[rows, :] - last * image


def shift(block, axis, distance):
    devices = range(lax.axis_size(axis))
    route = [(i - distance, i) for i in devices if i - distance in devices]
    return lax.ppermute(block, axis, route)


def exchange(t):
    return (
        shift(t[2], "sy", -1),
        shift(t[3], "sx", -1),
        shift(t[0], "sy", 1),
        shift(t[1], "sx", 1),
    )


def everywhere(blocks):
    return lax.all_to_all(blocks, BOTH, 0, 0, tiled=True)


def vertex_order(corner_map, rhs):
    names = corner_map[0]
    tags = names[None] + 1
    tail = jnp.pad(tags.astype(f32), ((0, 7), (0, R - tags.shape[1])))
    east, south = shift(tags, "sy", -1)[0], shift(tags, "sx", -1)[0]
    from_west = shift(jnp.concatenate([rhs[0], tail], 0), "sy", 1)
    from_north = shift(jnp.concatenate([rhs[1], tail], 0), "sx", 1)
    west, north = (x[CAP, : tags.shape[1]].astype(jnp.int32) for x in (from_west, from_north))

    def named(other):
        return jnp.any(tags[0][:, None] == other[None, :], axis=1)

    last_column = lax.axis_index("sy") == lax.axis_size("sy") - 1
    last_row = lax.axis_index("sx") == lax.axis_size("sx") - 1
    right = jnp.where(last_column, ~named(west), named(east)).astype(jnp.int32)
    lower = jnp.where(last_row, ~named(north), named(south)).astype(jnp.int32)
    vertex = right * 2 + lower
    before = (vertex[:, None] == vertex[None, :]) & (names[None, :] < names[:, None])
    row = vertex * 8 + jnp.sum(before.astype(jnp.int32), axis=1)
    order = (jnp.arange(32, dtype=jnp.int32)[:, None] == row[None, :]).astype(f32)
    return order, from_west, from_north


def on_device(
    jump_rhs, counts, slot_dof, remainder_inv, schur_matrix, coupling, coarse_local, corner_map
):
    rows, columns = lax.axis_size("sx"), lax.axis_size("sy")
    devices = rows * columns
    counts = counts[0]
    rhs = jump_rhs[0]
    order, west, north = vertex_order(corner_map, rhs)
    local = jnp.dot(jnp.dot(order, coarse_local[0], precision=highest), order.T, precision=highest)
    local = jnp.concatenate([local[v * 8 : v * 8 + 8] for v in range(4)], 1)
    row_dof, col_dof = slot_dof, slot_dof.reshape(NI, 1)
    matrix_outs = [((NI, NI), bf16), ((NI, NI), bf16)]
    sh, sl = call(permute_body, (schur_matrix[0], row_dof, col_dof), matrix_outs, MATRIX_SCRATCH, us=10.0, far=(0, 1))
    cpl, cpl_t = call(
        coupling_body, (coupling[0], order, row_dof), [((64, NI), bf16), ((NI, 128), bf16)], us=1.5, mib=12, out=(0, 1)
    )

    half, slab, longer = ((2 * CAP, R), f32), ((CAP, R), f32), ((CAP + 16, R), f32)
    few = ((8, R), f32)
    specs = lambda n, *far: [SM] + [HB if m in far else VM for m in range(1, n)]

    t = call(
        start_body,
        (counts, rhs, west, north, sh, sl, cpl),
        [longer] * 4,
        MATRIX_SCRATCH,
        specs(7, 4, 5),
        6.0,
        out=(0, 1, 2, 3),
    )
    row_dof, col_dof, local, *t = lax.optimization_barrier((row_dof, col_dof, local, *t))
    received = exchange(t)
    rh, rl = call(permute_body, (remainder_inv[0], row_dof, col_dof), matrix_outs, MATRIX_SCRATCH, us=10.0, far=(0, 1))
    blocks = everywhere(jnp.broadcast_to(local[None], (devices, 8, 128))).reshape(devices * 8, 128)
    (joined,) = call(joined_body, (cpl_t, *received), [((NI, 256), bf16)], us=1.0, mib=12, out=(0,))
    z0, out, *u = call(
        first_operator_body,
        (counts, *t, *received, rhs, rh, rl, cpl),
        [half, ((devices, 128), f32)] + [slab] * 4,
        MATRIX_SCRATCH,
        specs(13, 10, 11),
        7.0,
        out=(0, 2, 3, 4, 5),
    )
    arrived = everywhere(out.reshape(devices, 1, 128)).reshape(devices, 128)
    received = exchange(u)
    answer, state, factor = call(
        functools.partial(first_solve_body, rows, columns),
        (blocks, arrived),
        [((devices * 3, 128), f32), ((8, 128), f32), ((BLOCKS, 128, 768), bf16)],
        [
            *solve_scratch(),
            pltpu.VMEM((BLOCKS, 128, 128), f32),
            pltpu.VMEM((BLOCKS, 128, 256), f32),
        ],
        us=38.0,
        mib=16,
        far=(2,),
    )
    answer = everywhere(answer.reshape(devices, 1, 384)).reshape(devices * 3, 128)
    r1, w, first, *t = call(
        precondition_body,
        (counts, *u, *received, answer, joined, rhs, west, north, sh, sl),
        [half, half, few] + [slab] * 4,
        slab_scratch(8) + MATRIX_SCRATCH,
        specs(16, 1, 2, 3, 4, 5, 6, 7, 8, 14, 15),
        7.0,
        out=(0, 1),
    )
    received = exchange(t)
    z1, out, *u = call(
        second_operator_body,
        (counts, *t, *received, r1, w, rh, rl, cpl),
        [half, ((devices, 128), f32)] + [slab] * 4,
        MATRIX_SCRATCH,
        specs(14, 11, 12),
        7.0,
        out=(0, 2, 3, 4, 5),
    )
    arrived = everywhere(out.reshape(devices, 1, 128)).reshape(devices, 128)
    received = shift(u[2], "sy", -1), shift(u[3], "sx", -1)
    (answer,) = call(
        functools.partial(second_solve_body, rows, columns),
        (arrived, state, factor),
        [((devices * 3, 128), f32)],
        solve_scratch(),
        [VM, VM, HB],
        us=2.5,
        mib=12,
    )
    answer = everywhere(answer.reshape(devices, 1, 384)).reshape(devices * 3, 128)
    own = ((2, CAP, R), f32)
    multipliers, residual = call(
        end_body,
        (counts, u[0], u[1], *received, answer, joined, z0, z1, r1, w, first),
        [own, own],
        slab_scratch(4),
        specs(12, 1, 2, 3, 4),
        3.0,
    )
    return multipliers[None], residual[None]


def solution(mesh):
    four, three, two = P(BOTH, None, None, None), P(BOTH, None, None), P(BOTH, None)
    return jax.shard_map(
        on_device,
        mesh=mesh,
        in_specs=(four, two, two, three, three, three, three, two),
        out_specs=(four, four),
        check_vma=False,
    )
```

```python
import functools

import jax
import jax.numpy as jnp
from jax import lax
from jax.experimental import pallas as pl
from jax.experimental.pallas import tpu as pltpu
from jax.sharding import PartitionSpec as P

f32, bf16 = jnp.float32, jnp.bfloat16
highest = lax.Precision.HIGHEST
BOTH = ("sx", "sy")
CAP, R, NI = 256, 512, 1024
LEVELS = (
    (1, tuple(range(1, 16, 2))),
    (2, (2, 6, 10, 14)),
    (4, (4, 12)),
    (8, (0, 16)),
)
ROOT = 8
BLOCKS = 17
VM = pl.BlockSpec(memory_space=pltpu.VMEM)
SM = pl.BlockSpec(memory_space=pltpu.SMEM)
HB = pl.BlockSpec(memory_space=pltpu.HBM)


def call(body, ins, outs, scratch=(), specs=None, us=1.0, mib=24, far=(), out=()):
    return pl.pallas_call(
        body,
        out_shape=[
            pltpu.HBM(s, d) if n in far + out else jax.ShapeDtypeStruct(s, d) for n, (s, d) in enumerate(outs)
        ],
        in_specs=specs if specs is not None else [VM] * len(ins),
        out_specs=[HB if n in far else VM for n in range(len(outs))],
        scratch_shapes=list(scratch),
        cost_estimate=pl.CostEstimate(flops=int(us * 1.15e9), bytes_accessed=int(us * 1e6), transcendentals=0),
        compiler_params=pltpu.CompilerParams(vmem_limit_bytes=mib * 1024 * 1024),
    )(*[
        pltpu.with_memory_space_constraint(x, pltpu.HBM) if specs is not None and specs[n] is HB else x
        for n, x in enumerate(ins)
    ])


def dot(a, b):
    return jnp.dot(a, b, preferred_element_type=f32)


def split(x):
    hi = x.astype(bf16)
    return hi, (x - hi.astype(f32)).astype(bf16)


def iota(shape, axis):
    return lax.broadcasted_iota(jnp.int32, shape, axis)


MATRIX_SCRATCH = [
    pltpu.VMEM((NI, NI), bf16),
    pltpu.VMEM((NI, NI), bf16),
    pltpu.SemaphoreType.DMA((8,)),
]


def slab_copies(sources, targets, sems):
    return [
        [
            pltpu.make_async_copy(
                source.at[k * CAP : (k + 1) * CAP, :], target.at[k * CAP : (k + 1) * CAP, :], sems.at[k * 2 + n]
            )
            for n, (source, target) in enumerate(zip(sources, targets))
        ]
        for k in range(4)
    ]


class Matrix:
    def __init__(self, hi, lo, hi_here, lo_here, sems):
        self.here = hi_here, lo_here
        self.copies = slab_copies((hi, lo), self.here, sems)
        for pair in self.copies:
            for copy in pair:
                copy.start()

    def times(self, x, k):
        for copy in self.copies[k]:
            copy.wait()
        a, b = (part[k * CAP : (k + 1) * CAP, :] for part in self.here)
        xh, xl = x
        return dot(a, xh) + dot(a, xl) + dot(b, xh)


def permute_body(mat, row_dof, col_dof, hi_out, lo_out, hi_here, lo_here, sems):
    pick_t = jnp.where(iota((NI, NI), 0) == row_dof[...], 1.0, 0.0).astype(bf16)
    parts = split(mat[...])
    copies = slab_copies((hi_here, lo_here), (hi_out, lo_out), sems)
    for k in range(4):
        rows = slice(k * CAP, (k + 1) * CAP)
        pick = jnp.where(iota((CAP, NI), 1) == col_dof[rows, :], 1.0, 0.0).astype(bf16)
        for n, here in enumerate((hi_here, lo_here)):
            here[rows, :] = dot(dot(pick, parts[n]).astype(bf16), pick_t).astype(bf16)
            copies[k][n].start()
    for pair in copies:
        for copy in pair:
            copy.wait()


def coupling_body(coupling, order, row_dof, out, out_t):
    pick_t = jnp.where(iota((NI, NI), 0) == row_dof[...], 1.0, 0.0).astype(bf16)
    ranked = jnp.dot(order[...], coupling[...], precision=highest, preferred_element_type=f32)
    hi, lo = split(ranked)
    hi, lo = dot(hi, pick_t), dot(lo, pick_t)
    out[...] = jnp.concatenate([hi, lo], 0).astype(bf16)
    tall = jnp.concatenate([hi, hi, lo, jnp.zeros_like(lo)], 0)
    out_t[...] = tall.T.astype(bf16)


def neighbours(stride, pivot):
    left = pivot - stride if pivot - stride >= 0 else None
    right = pivot + stride if pivot + stride < BLOCKS else None
    return left, right


def coarse_body(rows, columns, x, factor, diag, side):
    lane8 = iota((8, 128), 1)
    sub8 = iota((8, 128), 0)
    r0, c0 = iota((128, 128), 0), iota((128, 128), 1)
    c72 = iota((72, 128), 1)
    start = jnp.where((r0 == c0) & (r0 % 8 >= 6) & (r0 < 72), 1.0, 0.0)
    for j in range(BLOCKS):
        diag[j] = start
        side[j] = jnp.zeros((128, 256), f32)

    def piece(tile, right_a, lower_a, right_b, r):
        offset = (right_a * 2 + lower_a) * 32 + right_b * 16
        moved = pltpu.roll(tile, (r * 8 - offset) % 128, 1)
        return jnp.where((lane8 >= r * 8) & (lane8 < r * 8 + 16), moved, 0.0)

    def gather(pair, _):
        for odd in (0, 1):
            c = pair * 2 + odd
            tiles = [x[pl.ds(pl.multiple_of((r * columns + c) * 8, 8), 8), :] for r in range(rows)]
            for right in (0, 1):
                for i in range(rows + 1):
                    acc = diag[c + right, i * 8 : i * 8 + 8, :]
                    for lower in (0, 1):
                        if 0 <= i - lower < rows:
                            acc = acc + piece(tiles[i - lower], right, lower, right, i - lower)
                    diag[c + right, i * 8 : i * 8 + 8, :] = acc
            right_a = 0 if odd else 1
            at = 128 if odd else 0
            for i in range(rows + 1):
                acc = jnp.zeros((8, 128), f32)
                for lower in (0, 1):
                    if 0 <= i - lower < rows:
                        acc = acc + piece(tiles[i - lower], right_a, lower, 1 - right_a, i - lower)
                side[pair * 2 + 1, i * 8 : i * 8 + 8, at : at + 128] = acc
        return 0

    lax.fori_loop(0, columns // 2, gather, 0)

    def invert(blocks):
        def eliminate(own, own_turned, inside, i):
            pivot = {
                (p, q): jnp.broadcast_to(own_turned[p : p + 1, q : q + 1], (8, 128))
                for p in range(6)
                for q in range(p, 6)
            }
            line = [
                jnp.where(
                    inside,
                    jnp.where(lane8 - i * 8 == p, 1.0, 0.0),
                    jnp.broadcast_to(own[p : p + 1, :], (8, 128)),
                )
                for p in range(6)
            ]
            for p in range(6):
                inverse = 1.0 / pivot[p, p]
                scaled = {q: pivot[p, q] * inverse for q in range(p + 1, 6)}
                line[p] = line[p] * inverse
                for q in range(6):
                    if q < p:
                        line[q] = line[q] - pivot[q, p] * line[p]
                        for c in range(p + 1, 6):
                            pivot[q, c] = pivot[q, c] - pivot[q, p] * scaled[c]
                    if q > p:
                        line[q] = line[q] - pivot[p, q] * line[p]
                        for c in range(q, 6):
                            pivot[q, c] = pivot[q, c] - pivot[p, q] * scaled[c]
                for q in range(p + 1, 6):
                    pivot[p, q] = scaled[q]
            return line

        table = [diag[j, 0:72, :] for j in blocks]
        own = [t[0:8, :] for t in table]
        for i in range(9):
            low, high = i * 8, i * 8 + 8
            inside = (lane8 >= low) & (lane8 < high)
            ahead = []
            for n, t in enumerate(table):
                line = eliminate(own[n], own[n][:, low:high], inside, i)
                wide = own[n]
                for p in range(6):
                    wide = jnp.where(sub8 == p, line[p], wide)
                next_own = None
                if i < 8:
                    next_old = t[high : high + 8, :]
                    next_own = jnp.where(inside, 0.0, next_old)
                    for p in range(6):
                        next_own = next_own - next_old[:, low + p : low + p + 1] * line[p]
                ahead.append(next_own)
                moved = jnp.dot(
                    t[:, low:high],
                    jnp.where(sub8 < 6, wide, 0.0),
                    precision=highest,
                    preferred_element_type=f32,
                )
                kept = jnp.where((c72 >= low) & (c72 < high), 0.0, t) - moved
                tiles = [kept[:low, :]] if i else []
                tiles.append(wide)
                if i < 8:
                    tiles.append(next_own)
                if i < 7:
                    tiles.append(kept[high + 8 :, :])
                table[n] = jnp.concatenate(tiles, 0)
            own = ahead
        for n, j in enumerate(blocks):
            diag[j, 0:72, :] = table[n]

    for level, (stride, pivots) in enumerate(LEVELS):
        invert(pivots)
        later = LEVELS[level + 1][1] if level + 1 < len(LEVELS) else ()
        for p in pivots:
            left, right = neighbours(stride, p)
            coupled = side[p]
            gain = jnp.dot(diag[p], coupled, precision=highest, preferred_element_type=f32)
            hi, lo = split(gain)
            factor[p, :, 256:] = jnp.concatenate([hi, lo], 1)
            schur = jnp.dot(coupled.T, gain, precision=highest, preferred_element_type=f32)
            if left is not None:
                diag[left] = diag[left] - schur[:128, :128]
            if right is not None:
                diag[right] = diag[right] - schur[128:, 128:]
            if left is not None and right is not None:
                if left in later:
                    side[left, :, 128:] = -schur[:128, 128:]
                else:
                    side[right, :, :128] = -schur[128:, :128]
    invert((ROOT,))
    factor[ROOT, :, 256:] = jnp.zeros((128, 512), bf16)
    for j in range(BLOCKS):
        hi, lo = split(diag[j])
        factor[j, :, :256] = jnp.concatenate([hi, lo], 1)


def row_times(x, hi, lo, transposed=False):
    high = x.astype(bf16).astype(f32)
    both = jnp.concatenate([high, x - high], 0).astype(bf16)
    dims = (((1,), (1 if transposed else 0,)), ((), ()))
    out = lax.dot_general(both, hi, dims, preferred_element_type=f32)
    out = out + lax.dot_general(both, lo, dims, preferred_element_type=f32)
    return out[:8] + out[8:]


def coarse_solve(rows, columns, w, factor, placed, solved, pending=None):
    lane16 = iota((16, 128), 1)
    placed[...] = jnp.zeros_like(placed)
    solved[...] = jnp.zeros_like(solved)
    for k in range(4):
        for right in (0, 1):
            offset = k * 32 + right * 16
            acc = jnp.zeros((16, 128), f32)
            for r in range(rows):
                moved = pltpu.roll(w[r * columns : (r + 1) * columns, :], (r * 8 - offset) % 128, 1)
                take = (lane16 >= r * 8) & (lane16 < r * 8 + 16) & (lane16 % 8 < 6)
                acc = acc + jnp.where(take, moved, 0.0)
            at = k * 24 + 1 + right
            placed[at : at + 16, :] = placed[at : at + 16, :] + acc
    b = [placed[pl.ds(j + 1, 8, stride=24), :] for j in range(BLOCKS)]
    if pending is not None:
        pending.wait()
    none = jnp.zeros((8, 128), f32)
    y, sol = [none] * BLOCKS, [none] * BLOCKS
    for stride, pivots in LEVELS:
        for p in pivots:
            left, right = neighbours(stride, p)
            gb = row_times(b[p], factor[p, :, 256:512], factor[p, :, 512:])
            if left is not None:
                b[left] = b[left] - gb[:, :128]
            if right is not None:
                b[right] = b[right] - gb[:, 128:]
            y[p] = row_times(b[p], factor[p, :, :128], factor[p, :, 128:256])
    sol[ROOT] = row_times(b[ROOT], factor[ROOT, :, :128], factor[ROOT, :, 128:256])
    for stride, pivots in LEVELS[::-1]:
        for p in pivots:
            left, right = neighbours(stride, p)
            pair = jnp.concatenate(
                [none if left is None else sol[left], none if right is None else sol[right]], 1
            )
            sol[p] = y[p] - row_times(pair, factor[p, :, 256:512], factor[p, :, 512:], True)
    for j in range(BLOCKS):
        solved[pl.ds(j + 1, 8, stride=24), :] = sol[j]
    product = placed[...] * solved[...]
    energy = [jnp.sum(product[k * 24 : k * 24 + 24, :], keepdims=True) for k in range(4)]
    answers = []
    for r in range(rows):
        own, beside, beyond = (jnp.zeros((16, 128), f32) for _ in range(3))

        def place(acc, k, column, source, offset, size):
            at = k * 24 + 1 + column
            moved = pltpu.roll(solved[at : at + 16, :], (offset - source * 8) % 128, 1)
            return acc + jnp.where((lane16 >= offset) & (lane16 < offset + size), moved, 0.0)

        for k in range(4):
            for right in (0, 1):
                own = place(own, k, right, r, k * 32 + right * 16, 16)
                beside = place(beside, k, (2, -1)[right], r, k * 32 + right * 16, 16)
                beyond = place(beyond, k, right, r + 2, k * 32 + right * 8, 8)
                if r > 0:
                    beyond = place(beyond, k, right, r - 1, k * 32 + 16 + right * 8, 8)
        answers.append((own, beside, beyond))
    return answers, energy


def lane_sum(total, at):
    lane = iota((1, 128), 1)
    return jnp.sum(jnp.where(lane == at, total, 0.0), axis=1, keepdims=True)


def by_case(values):
    lane = iota((1, 128), 1)
    out = jnp.zeros((1, 128), f32)
    for k in range(4):
        out = jnp.where(lane // 32 == k, values[k], out)
    return out


def write_answers(out, answers, columns, first, second):
    lane = iota((1, 128), 1)
    for r, (acc, beside, beyond) in enumerate(answers):
        acc = jnp.where(lane % 32 == 6, first, acc)
        acc = jnp.where(lane % 32 == 7, second, acc)
        for group, values in enumerate((acc, beside, beyond)):
            out[pl.ds(r * columns * 3 + group, 16, stride=3), :] = values


def first_solve_body(rows, columns, blocks, w, out, state, kept, factor, sem, placed, solved, diag, side):
    coarse_body(rows, columns, blocks, factor, diag, side)
    keep = pltpu.make_async_copy(factor, kept, sem)
    keep.start()
    answers, energy = coarse_solve(rows, columns, w, factor, placed, solved)
    total = jnp.sum(w[...], axis=0, keepdims=True)
    dots = by_case([lane_sum(total, k * 32 + 6) for k in range(4)])
    curvature = by_case([lane_sum(total, k * 32 + 7) + energy[k] for k in range(4)])
    state[...] = jnp.concatenate([dots, curvature, jnp.zeros((6, 128), f32)], 0)
    step = dots / curvature
    write_answers(out, answers, columns, step, step)
    keep.wait()


def second_solve_body(rows, columns, w, state, kept, out, factor, sem, placed, solved):
    bring = pltpu.make_async_copy(kept, factor, sem)
    bring.start()
    answers, energy = coarse_solve(rows, columns, w, factor, placed, solved, bring)
    total = jnp.sum(w[...], axis=0, keepdims=True)
    dots = by_case([lane_sum(total, k * 32 + 6) for k in range(4)])
    own = by_case([lane_sum(total, k * 32 + 7) + energy[k] for k in range(4)])
    cross = by_case([lane_sum(total, k * 32 + 14) for k in range(4)])
    ratio = dots / state[0:1, :]
    curvature = own + ratio * (2.0 * cross + ratio * state[1:2, :])
    write_answers(out, answers, columns, dots / curvature, ratio)


def solve_scratch():
    return [
        pltpu.VMEM((BLOCKS, 128, 768), bf16),
        pltpu.SemaphoreType.DMA,
        pltpu.VMEM((192, 128), f32),
        pltpu.VMEM((192, 128), f32),
    ]


def mask_of(counts, k):
    return iota((CAP, R), 0) < counts[k]


def residual_slots(counts, rhs, west, north, k):
    values = (rhs[0], rhs[1], None, None)[k] if k < 2 else -(west, north)[k - 2][:CAP, :]
    return jnp.where(mask_of(counts, k), values, 0.0)


def start_body(counts, rhs, west, north, hi, lo, coupling, t0, t1, t2, t3, *here):
    matrix = Matrix(hi, lo, *here)
    x = split(jnp.concatenate([residual_slots(counts, rhs, west, north, k) for k in range(4)], 0))
    rows = coupling[:32, :].astype(f32) + coupling[32:, :].astype(f32)
    for k, t in enumerate((t0, t1, t2, t3)):
        t[:CAP, :] = matrix.times(x, k)
        own = rows[:, k * CAP : (k + 1) * CAP]
        t[CAP:, :] = jnp.concatenate([own[:16, :], own[16:, :]], 1)


def joined_body(own_t, e0, e1, e2, e3, out):
    other = jnp.concatenate(
        [jnp.concatenate([e[CAP:, :CAP], e[CAP:, CAP:]], 0) for e in (e0, e1, e2, e3)], 1
    )
    hi = other.astype(bf16).astype(f32)
    lo = other - hi
    tall = jnp.concatenate([hi, hi, lo, jnp.zeros_like(lo)], 0)
    out[:, :128] = own_t[...]
    out[:, 128:] = (-tall.T).astype(bf16)


def jumped(counts, t, received, k):
    return jnp.where(mask_of(counts, k), t[k][:CAP, :] - received[k][:CAP, :], 0.0)


def payload(loads, rows_of_dots):
    sub = iota((32, R), 0)
    for at, values in rows_of_dots:
        loads = jnp.where(sub == at, values, loads)
    tall = jnp.concatenate([loads[:, k * 128 : (k + 1) * 128] for k in range(4)], 0)
    return tall.T


def corner_loads(coupling, x):
    xh, xl = x
    both = dot(coupling[...], xh)
    return both[:32] + both[32:] + dot(coupling[:32, :], xl)


def sum_rows(x):
    return jnp.sum(x, axis=0, keepdims=True)


def operate(counts, t, received, matrix, coupling, u):
    field = [jumped(counts, t, received, k) for k in range(4)]
    x = split(jnp.concatenate(field, 0))
    loads = corner_loads(coupling, x)
    energy = jnp.zeros((1, R), f32)
    for k in range(4):
        part = matrix.times(x, k)
        u[k][...] = part
        energy = energy + sum_rows(part * field[k])
    return field, loads, energy


def first_operator_body(
    counts, t0, t1, t2, t3, e0, e1, e2, e3, rhs, hi, lo, coupling,
    z, out, u0, u1, u2, u3, *here,
):
    matrix = Matrix(hi, lo, *here)
    u = (u0, u1, u2, u3)
    field, loads, energy = operate(counts, (t0, t1, t2, t3), (e0, e1, e2, e3), matrix, coupling, u)
    dots = jnp.zeros((1, R), f32)
    for k in range(2):
        z[k * CAP : (k + 1) * CAP, :] = field[k]
        dots = dots + sum_rows(rhs[k] * field[k])
    out[...] = payload(loads, ((6, dots), (7, energy)))


def second_operator_body(
    counts, t0, t1, t2, t3, e0, e1, e2, e3, r1, w4, hi, lo, coupling,
    z, out, u0, u1, u2, u3, slab_here, slab_sems, *here,
):
    matrix = Matrix(hi, lo, *here)
    top, bottom = slice(0, CAP), slice(CAP, 2 * CAP)
    slabs = Slabs(
        (r1.at[top, :], w4.at[top, :], r1.at[bottom, :], w4.at[bottom, :]), slab_here, slab_sems
    )
    u = (u0, u1, u2, u3)
    field, loads, energy = operate(counts, (t0, t1, t2, t3), (e0, e1, e2, e3), matrix, coupling, u)
    dots, cross = jnp.zeros((1, R), f32), jnp.zeros((1, R), f32)
    for k in range(2):
        rows = slice(k * CAP, (k + 1) * CAP)
        z[rows, :] = field[k]
        dots = dots + sum_rows(slabs[2 * k] * field[k])
        cross = cross + sum_rows(slabs[2 * k + 1] * field[k])
    out[...] = payload(loads, ((6, dots), (7, energy), (14, cross)))


def unpack(answer):
    flat = []
    for group in range(3):
        tall = answer[pl.ds(group, 128, stride=3), :].T
        flat.append(jnp.concatenate([tall[k * 32 : (k + 1) * 32, :] for k in range(4)], 1))
    scalars = flat[0][0:8, :]
    keep = iota((32, R), 0) % 8 < 6
    own, beside, beyond = (jnp.where(keep, x, 0.0) for x in flat)
    o = [own[v * 8 : v * 8 + 8, :] for v in range(4)]
    b = [beyond[v * 8 : v * 8 + 8, :] for v in range(4)]
    others = (
        jnp.concatenate([own[16:, :], beside[:16, :]], 0),
        jnp.concatenate([o[1], b[0], o[3], b[1]], 0),
        jnp.concatenate([beside[16:, :], own[:16, :]], 0),
        jnp.concatenate([b[2], o[0], b[3], o[2]], 0),
    )

    def parts(x):
        hi = x.astype(bf16).astype(f32)
        return [hi, x - hi, hi, jnp.zeros_like(hi)]

    mine = parts(own)
    return scalars, [jnp.concatenate(mine + parts(x), 0).astype(bf16) for x in others]


class Slabs:
    def __init__(self, sources, here, sems):
        self.here = here
        self.copies = [
            pltpu.make_async_copy(source, here.at[n], sems.at[n]) for n, source in enumerate(sources)
        ]
        for copy in self.copies:
            copy.start()

    def __getitem__(self, n):
        self.copies[n].wait()
        return self.here[n]


def slab_scratch(n):
    return [pltpu.VMEM((n, CAP, R), f32), pltpu.SemaphoreType.DMA((n,))]


def image_of(counts, slabs, joined, sides, k):
    across = dot(joined[k * CAP : (k + 1) * CAP, :], sides[k])
    return jnp.where(mask_of(counts, k), slabs[2 * k] - slabs[2 * k + 1] + across, 0.0)


def precondition_body(
    counts, u0, u1, u2, u3, e0, e1, e2, e3, answer, joined, rhs, west, north, hi, lo,
    r1, w, scalars, s0, s1, s2, s3, slab_here, slab_sems, *here,
):
    slabs = Slabs((u0, e0, u1, e1, u2, e2, u3, e3), slab_here, slab_sems)
    matrix = Matrix(hi, lo, *here)
    first, sides = unpack(answer)
    scalars[...] = first
    step = first[6:7, :]
    work = []
    for k in range(4):
        image = image_of(counts, slabs, joined, sides, k)
        work.append(residual_slots(counts, rhs, west, north, k) - step * image)
        if k < 2:
            w[k * CAP : (k + 1) * CAP, :] = image
            r1[k * CAP : (k + 1) * CAP, :] = work[k]
    x = split(jnp.concatenate(work, 0))
    for k, out in enumerate((s0, s1, s2, s3)):
        out[...] = matrix.times(x, k)


def end_body(counts, u0, u1, e0, e1, answer, joined, z4, z1, r1, w, first, mult, residual, *here):
    slabs = Slabs((u0, e0, u1, e1), *here)
    second, sides = unpack(answer)
    step, last, ratio = first[6:7, :], second[6:7, :], second[7:8, :]
    for k in range(2):
        rows = slice(k * CAP, (k + 1) * CAP)
        start = z4[rows, :]
        mult[k] = step * start + last * (z1[rows, :] + ratio * start)
        image = image_of(counts, slabs, joined, sides, k) + ratio * w[rows, :]
        residual[k] = r1[rows, :] - last * image


def shift(block, axis, distance):
    devices = range(lax.axis_size(axis))
    route = [(i - distance, i) for i in devices if i - distance in devices]
    return lax.ppermute(block, axis, route)


def exchange(t):
    return (
        shift(t[2], "sy", -1),
        shift(t[3], "sx", -1),
        shift(t[0], "sy", 1),
        shift(t[1], "sx", 1),
    )


def everywhere(blocks):
    return lax.all_to_all(blocks, BOTH, 0, 0, tiled=True)


def vertex_order(corner_map, rhs):
    names = corner_map[0]
    tags = names[None] + 1
    tail = jnp.pad(tags.astype(f32), ((0, 7), (0, R - tags.shape[1])))
    east, south = shift(tags, "sy", -1)[0], shift(tags, "sx", -1)[0]
    from_west = shift(jnp.concatenate([rhs[0], tail], 0), "sy", 1)
    from_north = shift(jnp.concatenate([rhs[1], tail], 0), "sx", 1)
    west, north = (x[CAP, : tags.shape[1]].astype(jnp.int32) for x in (from_west, from_north))

    def named(other):
        return jnp.any(tags[0][:, None] == other[None, :], axis=1)

    last_column = lax.axis_index("sy") == lax.axis_size("sy") - 1
    last_row = lax.axis_index("sx") == lax.axis_size("sx") - 1
    right = jnp.where(last_column, ~named(west), named(east)).astype(jnp.int32)
    lower = jnp.where(last_row, ~named(north), named(south)).astype(jnp.int32)
    vertex = right * 2 + lower
    before = (vertex[:, None] == vertex[None, :]) & (names[None, :] < names[:, None])
    row = vertex * 8 + jnp.sum(before.astype(jnp.int32), axis=1)
    order = (jnp.arange(32, dtype=jnp.int32)[:, None] == row[None, :]).astype(f32)
    return order, from_west, from_north


def on_device(
    jump_rhs, counts, slot_dof, remainder_inv, schur_matrix, coupling, coarse_local, corner_map
):
    rows, columns = lax.axis_size("sx"), lax.axis_size("sy")
    devices = rows * columns
    counts = counts[0]
    rhs = jump_rhs[0]
    order, west, north = vertex_order(corner_map, rhs)
    local = jnp.dot(jnp.dot(order, coarse_local[0], precision=highest), order.T, precision=highest)
    local = jnp.concatenate([local[v * 8 : v * 8 + 8] for v in range(4)], 1)
    row_dof, col_dof = slot_dof, slot_dof.reshape(NI, 1)
    matrix_outs = [((NI, NI), bf16), ((NI, NI), bf16)]
    sh, sl = call(permute_body, (schur_matrix[0], row_dof, col_dof), matrix_outs, MATRIX_SCRATCH, us=10.0, far=(0, 1))
    cpl, cpl_t = call(
        coupling_body, (coupling[0], order, row_dof), [((64, NI), bf16), ((NI, 128), bf16)], us=1.5, mib=12, out=(0, 1)
    )

    half, slab, longer = ((2 * CAP, R), f32), ((CAP, R), f32), ((CAP + 16, R), f32)
    few = ((8, R), f32)
    specs = lambda n, *far: [SM] + [HB if m in far else VM for m in range(1, n)]

    t = call(
        start_body,
        (counts, rhs, west, north, sh, sl, cpl),
        [longer] * 4,
        MATRIX_SCRATCH,
        specs(7, 4, 5),
        6.0,
        out=(0, 1, 2, 3),
    )
    row_dof, col_dof, local, *t = lax.optimization_barrier((row_dof, col_dof, local, *t))
    received = exchange(t)
    rh, rl = call(permute_body, (remainder_inv[0], row_dof, col_dof), matrix_outs, MATRIX_SCRATCH, us=10.0, far=(0, 1))
    blocks = everywhere(jnp.broadcast_to(local[None], (devices, 8, 128))).reshape(devices * 8, 128)
    (joined,) = call(joined_body, (cpl_t, *received), [((NI, 256), bf16)], us=1.0, mib=12, out=(0,))
    z0, out, *u = call(
        first_operator_body,
        (counts, *t, *received, rhs, rh, rl, cpl),
        [half, ((devices, 128), f32)] + [slab] * 4,
        MATRIX_SCRATCH,
        specs(13, 10, 11),
        7.0,
        out=(0, 2, 3, 4, 5),
    )
    arrived = everywhere(out.reshape(devices, 1, 128)).reshape(devices, 128)
    received = exchange(u)
    answer, state, factor = call(
        functools.partial(first_solve_body, rows, columns),
        (blocks, arrived),
        [((devices * 3, 128), f32), ((8, 128), f32), ((BLOCKS, 128, 768), bf16)],
        [
            *solve_scratch(),
            pltpu.VMEM((BLOCKS, 128, 128), f32),
            pltpu.VMEM((BLOCKS, 128, 256), f32),
        ],
        us=38.0,
        mib=16,
        far=(2,),
    )
    answer = everywhere(answer.reshape(devices, 1, 384)).reshape(devices * 3, 128)
    r1, w, first, *t = call(
        precondition_body,
        (counts, *u, *received, answer, joined, rhs, west, north, sh, sl),
        [half, half, few] + [slab] * 4,
        slab_scratch(8) + MATRIX_SCRATCH,
        specs(16, 1, 2, 3, 4, 5, 6, 7, 8, 14, 15),
        7.0,
        out=(0, 1),
    )
    received = exchange(t)
    z1, out, *u = call(
        second_operator_body,
        (counts, *t, *received, r1, w, rh, rl, cpl),
        [half, ((devices, 128), f32)] + [slab] * 4,
        slab_scratch(4) + MATRIX_SCRATCH,
        specs(14, 9, 10, 11, 12),
        7.0,
        out=(0, 2, 3, 4, 5),
    )
    arrived = everywhere(out.reshape(devices, 1, 128)).reshape(devices, 128)
    received = shift(u[2], "sy", -1), shift(u[3], "sx", -1)
    (answer,) = call(
        functools.partial(second_solve_body, rows, columns),
        (arrived, state, factor),
        [((devices * 3, 128), f32)],
        solve_scratch(),
        [VM, VM, HB],
        us=2.5,
        mib=12,
    )
    answer = everywhere(answer.reshape(devices, 1, 384)).reshape(devices * 3, 128)
    own = ((2, CAP, R), f32)
    multipliers, residual = call(
        end_body,
        (counts, u[0], u[1], *received, answer, joined, z0, z1, r1, w, first),
        [own, own],
        slab_scratch(4),
        specs(12, 1, 2, 3, 4),
        3.0,
    )
    return multipliers[None], residual[None]


def solution(mesh):
    four, three, two = P(BOTH, None, None, None), P(BOTH, None, None), P(BOTH, None)
    return jax.shard_map(
        on_device,
        mesh=mesh,
        in_specs=(four, two, two, three, three, three, three, two),
        out_specs=(four, four),
        check_vma=False,
    )
```
